512 devices in a mesh: section: 2 (over core), seq: 32 (over y_lo, z), tensor: 8 (over x, y_hi).
Axes of the slice: x: 4, y: 4 (y_hi: 2, y_lo: 2; y = y_hi * 2 + y_lo), z: 16, core: 2. Of those that a mesh axis runs over, the one named last changes fastest.
Arguments:
- queries: bfloat16 [65536, 4096], P(('section', 'seq'), 'tensor'), may hold values from -18 to 18
- store_kv: bfloat16 [2, 24576, 4096], P(None, ('section', 'seq'), 'tensor'), may hold values from -6 to 6
- out_grad: bfloat16 [65536, 4096], P(('section', 'seq'), 'tensor'), may hold values from -48 to 48
- neighbour_owner: int32 [1024, 2], P(('section', 'seq', 'tensor')), may hold values from 0 to 31, all different within a row; in each aligned block of 16 rows (0 to 15, 16 to 31, ...) at most 2 rows name the same one
- neighbour_slot: int32 [1024, 2], P(('section', 'seq', 'tensor')), may hold values from 0 to 2
- neighbour_count: int32 [1024], P(('section', 'seq', 'tensor')), may hold values from 1 to 2
Outputs:
- attended: bfloat16 [65536, 4096], P(('section', 'seq'), 'tensor')
- store_grad: bfloat16 [2, 24576, 4096], P(None, ('section', 'seq'), 'tensor')
The draws below stay inside these ranges and needn't reach their ends.
Inputs may be any that keep to these rules, and one draw needn't show every extreme that they name: `neighbour_owner`: each span names 2 different owners. Among the 16 spans of one device (aligned blocks of rows), no owner is named more than 2 times; that many is reached in some blocks.
All inputs are finite; a program needn't handle non-finite values.
Results may differ from the reference program's by a relative error of at most 0.0065.
Values may be sent and summed in bfloat16 or wider, within the bound.
A program may use at most 128 MiB of HBM per device.

```python
import math
import jax
import jax.numpy as jnp
import numpy as np
from jax import lax

HEADS = 32
HEAD_DIM = 128
SPAN = 64
NLEN = 128
NEIGH = 2
CH_DEV = 16
NB_DEV = 3
CAP = 2
HW = 4096
SPANS = 1024
TOKENS = 65536
STORE_ROWS = 24576
N_SECTION = 2
N_SEQ = 32


def draw_queries(key, part):
    key = jax.random.fold_in(key, 11)
    return jax.random.truncated_normal(key, -6.0, 6.0, (TOKENS, HW), jnp.float32).astype(jnp.bfloat16)


def draw_store_kv(key, part):
    key = jax.random.fold_in(key, 12)
    return jax.random.truncated_normal(key, -6.0, 6.0, (2, STORE_ROWS, HW), jnp.float32).astype(jnp.bfloat16)


def draw_neighbour_count(key, part):
    key = jax.random.fold_in(key, 13)
    raw = jax.random.randint(key, (SPANS,), 0, 4)
    counts = 1 + jnp.minimum(raw, 1)
    counts = counts.at[0].set(1).at[1].set(2)
    return counts.astype(jnp.int32)


def set_ends(values, stream_key, least, largest):
    spot = [jax.random.randint(jax.random.fold_in(stream_key, axis), (), 0, length) for axis, length in enumerate(values.shape)]
    longest = values.shape.index(max(values.shape))
    beside = spot[:longest] + [(spot[longest] + 1) % values.shape[longest]] + spot[longest + 1:]
    return values.at[tuple(spot)].set(least).at[tuple(beside)].set(largest)


def levels(own_key, dims, pieces, low, largest):
    factor_of, own = 1.0, jax.random.fold_in(own_key, 6)
    for position, blocks in pieces:
        steps = jnp.exp(jax.random.uniform(jax.random.fold_in(own, position), (blocks,), jnp.float32, low / len(pieces), largest / len(pieces)))
        factor_of = factor_of * jnp.repeat(steps, dims[position] // blocks).reshape([-1 if axis == position else 1 for axis in range(len(dims))])
    return factor_of


def shared_out(stream_key, own, number, rows, count, top, most, slope):
    order = jax.random.permutation(stream_key, count)
    packed, common = portions_of(count, rows * top, most, slope, True), portions_of(count, rows * top, most, slope, False)
    places = jnp.arange(count)

    def named(sizes, offset_by):
        used = int((sizes > 0).sum())
        fixed = max(1, used // 4)
        passed = fixed + (places - fixed + offset_by * (used - fixed)) % max(1, count - fixed)
        return jnp.zeros((count,), jnp.int32).at[order[jnp.where(places < fixed, places, passed)]].set(jnp.asarray(sizes, jnp.int32))

    sizes = jnp.where(number % 4 == 0, named(packed, number // 4), named(common, number - number // 4 - 1))
    mixed = jax.random.permutation(jax.random.fold_in(own, 3), count)
    source_of, sink = mixed[0:count // 2 * 2:2], mixed[1:count // 2 * 2:2]
    margin = jnp.minimum(sizes[source_of] - 1, most - sizes[sink]) // 2
    margin = jnp.where((source_of == order[0]) | (sink == order[0]) | (sizes[sink] == 0), 0, jnp.maximum(margin, 0))
    passed = jax.random.randint(jax.random.fold_in(own, 4), (count // 2,), 0, 1 << 20) % (margin + 1)
    sizes = sizes.at[source_of].add(-passed).at[sink].add(passed)
    members = jnp.searchsorted(jnp.cumsum(sizes), jnp.arange(rows * top), side="right").astype(jnp.int32)
    listing = members.reshape(top, rows).T
    listing = listing[jax.random.permutation(jax.random.fold_in(own, 1), rows)]
    offset_by = jax.random.randint(jax.random.fold_in(own, 2), (rows, 1), 0, top)
    return jnp.take_along_axis(listing, (jnp.arange(top)[None, :] + offset_by) % top, axis=1)


def portions_of(count, total, bound, skew, full):
    portions = [(1 << 20) // math.isqrt(rank ** skew) + 1 for rank in range(1, count + 1)]
    largest = bound if full else min(bound, max(-(-total // count), total * portions[0] // sum(portions)))
    least = 1 if total - largest >= count - 1 else 0
    given, spare = [largest] + [least] * (count - 1), total - largest - least * (count - 1)
    while spare > 0:
        free = [i for i in range(1, count) if given[i] < largest] or [i for i in range(1, count) if given[i] < bound]
        whole, remaining = sum([portions[i] for i in free]), spare
        for i in free:
            extra = min(bound - given[i], max(1, remaining * portions[i] // whole), spare)
            given[i] = given[i] + extra
            spare = spare - extra
    return np.array(given)


def normal_values(own_key, dims, deviation, most, pieces=(), kind=jnp.bfloat16):
    result = jax.random.normal(own_key, dims, jnp.float32) * deviation
    if len(pieces) > 0:
        result = levels(own_key, dims, pieces, -0.22, 0.18) * result
    return jnp.clip(result, min=-most, max=most).astype(kind)


def setup_inputs(seed: int = 0) -> dict:
    arg_keys = jax.random.split(jax.random.key(seed), 7)
    queries = draw_queries(jax.random.fold_in(arg_keys[6], 71), 0)
    store_kv = draw_store_kv(jax.random.fold_in(arg_keys[6], 71), 0)
    out_grad = normal_values(arg_keys[2], (TOKENS, HW), 8.0, 48.0, ((0, 64), (1, 8)))
    neighbour_owner_keys = jax.random.split(jax.random.fold_in(arg_keys[3], 1), SPANS // CH_DEV)
    neighbour_owner_turns = jax.random.permutation(jax.random.fold_in(arg_keys[3], 3), SPANS // CH_DEV)
    neighbour_owner = jax.vmap(lambda own, number: shared_out(jax.random.fold_in(arg_keys[3], 2), own, number, CH_DEV, N_SEQ, NEIGH, CAP, 2))(neighbour_owner_keys, neighbour_owner_turns).reshape((SPANS, NEIGH))
    neighbour_slot = set_ends(jax.random.randint(arg_keys[4], (SPANS, NEIGH), 0, NB_DEV), jax.random.fold_in(arg_keys[4], 1), 0, NB_DEV - 1).astype(jnp.int32)
    neighbour_count = draw_neighbour_count(jax.random.fold_in(arg_keys[6], 71), 0)
    return {"queries": queries, "store_kv": store_kv, "out_grad": out_grad, "neighbour_owner": neighbour_owner, "neighbour_slot": neighbour_slot, "neighbour_count": neighbour_count}


far_below = -1e30


def rounded(values):
    return lax.optimization_barrier(values.astype(jnp.bfloat16)).astype(jnp.float32)


def reference(queries, store_kv, out_grad, neighbour_owner, neighbour_slot, neighbour_count):
    groups = N_SECTION * N_SEQ
    spans = CH_DEV * groups
    scaling = HEAD_DIM ** -0.5
    query_spans = queries.reshape(spans, SPAN, HEADS, HEAD_DIM)
    grad_spans = out_grad.reshape(spans, SPAN, HEADS, HEAD_DIM)
    key_store = store_kv[0].reshape(groups * NB_DEV, NLEN, HEADS, HEAD_DIM)
    value_store = store_kv[1].reshape(groups * NB_DEV, NLEN, HEADS, HEAD_DIM)
    span_ids = jnp.arange(spans, dtype=jnp.int32)
    section_of = span_ids // (CH_DEV * N_SEQ)
    entries = (((1 - section_of)[:, None] * N_SEQ + neighbour_owner) * NB_DEV + neighbour_slot).astype(jnp.int32)
    live_all = jnp.arange(NEIGH, dtype=jnp.int32)[None, :] < neighbour_count[:, None]

    def one_span(carry, inputs):
        grad_keys, grad_values = carry
        query_rows, grad_rows, entry_ids, live_flags = inputs
        query_f = query_rows.astype(jnp.float32)
        grad_f = grad_rows.astype(jnp.float32)
        keys_f = key_store[entry_ids].astype(jnp.float32)
        values_f = value_store[entry_ids].astype(jnp.float32)
        scores = jnp.einsum("qhd,jkhd->jhqk", query_f, keys_f, precision=lax.Precision.HIGHEST) * scaling
        row_max = jnp.max(scores, axis=-1, keepdims=True)
        local_lse = row_max[..., 0] + jnp.log(jnp.sum(jnp.exp(scores - row_max), axis=-1))
        weights = rounded(jnp.exp(scores - local_lse[..., None]))
        partial_value = rounded(jnp.einsum("jhqk,jkhd->jqhd", weights, values_f, precision=lax.Precision.HIGHEST))
        flags = live_flags[:, None, None]
        masked = jnp.where(flags, local_lse, far_below)
        row_top = jnp.max(masked, axis=0)
        lse_total = row_top + jnp.log(jnp.sum(jnp.where(flags, jnp.exp(masked - row_top), 0.0), axis=0))
        mixing = jnp.where(flags, jnp.exp(masked - lse_total), 0.0)
        attended = jnp.einsum("jhq,jqhd->qhd", mixing, partial_value, precision=lax.Precision.HIGHEST)
        attended_low = rounded(attended)
        delta = jnp.sum(grad_f * attended_low, axis=-1)
        prob = jnp.where(flags[..., None], jnp.exp(scores - lse_total[None, :, :, None]), 0.0)
        value_grad = jnp.einsum("jhqk,qhd->jkhd", rounded(prob), grad_f, precision=lax.Precision.HIGHEST)
        prob_grad = jnp.einsum("qhd,jkhd->jhqk", grad_f, values_f, precision=lax.Precision.HIGHEST)
        score_grad = rounded(prob * (prob_grad - jnp.transpose(delta)[None, :, :, None]))
        key_grad = jnp.einsum("jhqk,qhd->jkhd", score_grad, query_f, precision=lax.Precision.HIGHEST) * scaling
        grad_keys = grad_keys.at[entry_ids].add(key_grad)
        grad_values = grad_values.at[entry_ids].add(value_grad)
        return (grad_keys, grad_values), attended.astype(jnp.bfloat16)

    start = (jnp.zeros((groups * NB_DEV, NLEN, HEADS, HEAD_DIM), jnp.float32),
             jnp.zeros((groups * NB_DEV, NLEN, HEADS, HEAD_DIM), jnp.float32))
    (grad_keys, grad_values), attended = lax.scan(one_span, start, (query_spans, grad_spans, entries, live_all))
    store_grad = jnp.stack([grad_keys, grad_values]).reshape(2, STORE_ROWS, HW).astype(jnp.bfloat16)
    return attended.reshape(TOKENS, HW), store_grad
```

```python
import functools

import jax
import jax.numpy as jnp
from jax import lax
from jax.experimental import pallas as pl
from jax.experimental.pallas import tpu as pltpu
from jax.sharding import PartitionSpec as P

HEAD_DIM = 128
SPAN = 64
NLEN = 128
NEIGH = 2
SLOTS = 4
MESH = pl.DeviceIdType.MESH
DEAD = -1e30
NONE = -100000


def kernel(nz, ch, heads, tab, q_in, kv_in, g_in, att_out, sg_out,
           kv, q_own, q_nbr, g_own, g_nbr, pb, dpb, rs, fin, asend, arecv, att,
           lse, gp, st_s, st_r, wts, dlt,
           ag_s, ag_r, loc_s, loc_r, qg_s, qg_r, own_l, stx_s, stx_r,
           rs_s, rs_r, a_s, a_r, f_s, f_r, o_l):
    half = nz // 2
    stride = 2 * ch
    slots = nz * SLOTS
    scaling = HEAD_DIM ** (-0.5)
    q_blk, g_blk = (q_own, q_nbr), (g_own, g_nbr)
    sec = lax.axis_index("section")
    seq = lax.axis_index("seq")
    y, z = lax.div(seq, nz), lax.rem(seq, nz)
    up, down = lax.rem(z + 1, nz), lax.rem(z + nz - 1, nz)
    z_to = (up, down)

    def dev(s, yy, zz):
        return {"section": s, "seq": yy * nz + zz}

    sibling = dev(1 - sec, y, z)
    y_nbr = dev(sec, 1 - y, z)

    def remote(src, dst, ssem, rsem, device):
        return pltpu.make_async_remote_copy(
            src_ref=src, dst_ref=dst, send_sem=ssem, recv_sem=rsem,
            device_id=device, device_id_type=MESH)

    barrier = pltpu.get_barrier_semaphore()
    for device in (sibling, y_nbr, dev(sec, y, up), dev(sec, y, down),
                   dev(1 - sec, y, up), dev(1 - sec, y, down)):
        pl.semaphore_signal(barrier, inc=1, device_id=device, device_id_type=MESH)
    own_q = pltpu.make_async_copy(q_in, q_own, own_l.at[0])
    own_g = pltpu.make_async_copy(g_in, g_own, own_l.at[1])
    own_q.start()
    own_g.start()
    pl.semaphore_wait(barrier, 6)

    def place(d, k):
        return nz - k if d == 0 else k

    def first(d, c):
        return remote(kv_in.at[c], kv.at[c, place(d, 1)], ag_s.at[d, c, 1], ag_r.at[d, c, 1],
                      dev(1 - sec, y, z_to[d]))

    def forward(d, c, k):
        return remote(kv.at[c, place(d, k - 1)], kv.at[c, place(d, k)], ag_s.at[d, c, k],
                      ag_r.at[d, c, k], dev(sec, y, z_to[d]))

    def arrived(d, c, k):
        here = kv.at[c, place(d, k)]
        remote(here, here, ag_s.at[d, c, k], ag_r.at[d, c, k], dev(sec, y, z_to[d])).wait_recv()

    first(0, 0).start()
    first(1, 1).start()
    first(0, 1).start()
    first(1, 0).start()
    locals_ = [remote(kv_in.at[c], kv.at[c, 0], loc_s.at[c], loc_r.at[c], sibling) for c in (0, 1)]
    for copy in locals_:
        copy.start()
    swap = [remote(q_in, q_nbr, qg_s.at[0], qg_r.at[0], y_nbr),
            remote(g_in, g_nbr, qg_s.at[1], qg_r.at[1], y_nbr)]
    for copy in swap:
        copy.start()

    lse[...] = jnp.full_like(lse, DEAD)
    gp[...] = jnp.zeros_like(gp)
    for d, c, m in ((0, 0, half), (1, 1, half), (0, 1, half - 1), (1, 0, half - 1)):
        rs[d, c, m] = jnp.zeros(rs.shape[3:], rs.dtype)
    lanes = lax.broadcasted_iota(jnp.int32, (SPAN, 128), 1)

    def pick(three, es):
        return jnp.where(es == 0, three[0], jnp.where(es == 1, three[1], three[2]))

    def fwd_item(n, b):
        idx = jnp.where(lax.rem(n, 2) == 1, nz - lax.div(n + 1, 2), lax.div(n, 2))
        for r in (0, 1):
            sl = idx * SLOTS + (b * 2 + r)
            sp, es = tab[sl], tab[slots + sl]
            l_of = (tab[2 * slots + sl], tab[3 * slots + sl])
            stat_l, stat_g = [], []
            for h in range(heads):
                hs = pl.ds(h * HEAD_DIM, HEAD_DIM)
                qv = q_blk[b][sp, :, hs]
                gv = g_blk[b][sp, :, hs]
                ks = pick([kv[0, idx, e, :, hs] for e in range(3)], es)
                vs = pick([kv[1, idx, e, :, hs] for e in range(3)], es)
                s = lax.dot_general(qv, ks, (((1,), (1,)), ((), ())),
                                    preferred_element_type=jnp.float32) * scaling
                dp = lax.dot_general(gv, vs, (((1,), (1,)), ((), ())),
                                     preferred_element_type=jnp.float32)
                top = jnp.max(s, axis=1, keepdims=True)
                p = jnp.exp(s - top)
                tot = jnp.sum(p, axis=1, keepdims=True)
                p = p * (1.0 / tot)
                pb[sl, :, hs] = p
                dpb[sl, :, hs] = dp
                stat_l.append(top + jnp.log(tot))
                stat_g.append(jnp.sum(p * dp, axis=1, keepdims=True))
            for j in range(NEIGH):
                a, g2 = lse[j], gp[j]
                for h in range(heads):
                    hit = lanes == l_of[j] + h * stride
                    a = jnp.where(hit, stat_l[h], a)
                    g2 = jnp.where(hit, stat_g[h], g2)
                lse[j] = a
                gp[j] = g2

    def items(lo, hi, b):
        lax.fori_loop(lo, hi, lambda n, t: (fwd_item(n, b), t)[1], 0)

    own_q.wait()
    own_g.wait()
    for copy in locals_:
        copy.wait_recv()
    lag = min(4, half)

    def nbr_done(k):
        return jnp.minimum(jnp.maximum((k + 1 - lag) * 4, 0), 2 * half - 3)

    def gather_step(k, t):
        for d, c in ((0, 0), (1, 1)):
            arrived(d, c, k)
            forward(d, c, k + 1).start()
        items(jnp.maximum(2 * k - 3, 0), 2 * k - 1, 0)
        for d, c in ((0, 1), (1, 0)):
            arrived(d, c, k)

            @pl.when(k + 1 < half)
            def _():
                forward(d, c, k + 1).start()

        @pl.when(k == lag)
        def _():
            for copy in swap:
                copy.wait_recv()

        items(nbr_done(k - 1), nbr_done(k), 1)
        return t

    lax.fori_loop(1, half, gather_step, 0)
    if half <= lag:
        for copy in swap:
            copy.wait_recv()
    items(2 * half - 3, 2 * half - 1, 0)
    items(nbr_done(half - 1), 2 * half - 1, 1)
    arrived(0, 0, half)
    arrived(1, 1, half)
    fwd_item(2 * half - 1, 0)
    fwd_item(2 * half - 1, 1)

    a0, a1 = lse[0], lse[1]
    top = jnp.maximum(a0, a1)
    lc = top + jnp.log(jnp.exp(a0 - top) + jnp.exp(a1 - top))
    gc = jnp.exp(a0 - lc) * gp[0] + jnp.exp(a1 - lc) * gp[1]
    st_s[0] = lc
    st_s[1] = gc
    stats = remote(st_s, st_r, stx_s.at[0], stx_r.at[0], y_nbr)
    stats.start()
    stats.wait_recv()
    lo_, go_ = st_r[0], st_r[1]
    top = jnp.maximum(lc, lo_)
    total = top + jnp.log(jnp.exp(lc - top) + jnp.exp(lo_ - top))
    dlt[...] = jnp.exp(lc - total) * gc + jnp.exp(lo_ - total) * go_
    wts[0] = jnp.exp(a0 - total)
    wts[1] = jnp.exp(a1 - total)

    def column(values, lane):
        return jnp.sum(jnp.where(lanes == lane, values, 0.0), axis=1, keepdims=True)

    def contribution(c, idx, h):
        hs = pl.ds(h * HEAD_DIM, HEAD_DIM)
        left, right = [], []
        for slot in range(SLOTS):
            b = slot // 2
            sl = idx * SLOTS + slot
            sp, es = tab[sl], tab[slots + sl]
            l0 = tab[2 * slots + sl] + h * stride
            l1 = tab[3 * slots + sl] + h * stride
            w = jnp.where(lanes == l0, wts[0], 0.0) + jnp.where(lanes == l1, wts[1], 0.0)
            p = pb[sl, :, hs] * jnp.sum(w, axis=1, keepdims=True)
            if c == 0:
                p = p * (dpb[sl, :, hs] - column(dlt[...], jnp.maximum(l0, l1)))
                right.append(q_blk[b][sp, :, hs])
            else:
                right.append(g_blk[b][sp, :, hs])
            x = p.astype(jnp.bfloat16)
            zero = jnp.zeros_like(x)
            left.append(jnp.concatenate([jnp.where(es == e, x, zero) for e in range(3)], axis=1))
        out = lax.dot_general(jnp.concatenate(left, axis=0), jnp.concatenate(right, axis=0),
                              (((0,), (0,)), ((), ())), preferred_element_type=jnp.float32)
        if c == 0:
            out = out * scaling
        return out.reshape(3, NLEN, HEAD_DIM)

    def step_on(d, c, m):
        zz = lax.rem(z + 1 + d * (nz - 2), nz)
        return remote(rs.at[d, c, m], rs.at[d, c, m - 1], rs_s.at[d, c, m - 1],
                      rs_r.at[d, c, m - 1], dev(sec, y, zz))

    def sum_arrived(d, c, m):
        here = rs.at[d, c, m]
        remote(here, here, rs_s.at[d, c, m], rs_r.at[d, c, m], y_nbr).wait_recv()

    def chunk(d, c, m):
        idx = jnp.where(d == 0, m, nz - m)
        for h in range(heads):
            hs = pl.ds(h * HEAD_DIM, HEAD_DIM)
            o = contribution(c, idx, h) + rs[d, c, m, :, :, hs].astype(jnp.float32)
            rs[d, c, m, :, :, hs] = o.astype(jnp.bfloat16)
        step_on(d, c, m).start()

    def attended_span(b, sp):
        y_b = y if b == 0 else 1 - y
        outs = []
        for h in range(heads):
            hs = pl.ds(h * HEAD_DIM, HEAD_DIM)
            acc = jnp.zeros((SPAN, HEAD_DIM), jnp.float32)
            for j in range(NEIGH):
                at = 4 * slots + (b * ch + sp) * NEIGH + j
                sl = tab[at]
                idx = tab[at + 2 * ch * NEIGH]
                es = tab[at + 4 * ch * NEIGH]
                w = column(wts[j], y_b * ch + sp + h * stride)
                p = (pb[sl, :, hs] * w).astype(jnp.bfloat16)
                acc += jnp.dot(p, kv[1, idx, es, :, hs], preferred_element_type=jnp.float32)
            outs.append((hs, acc))
        return outs

    def nbr_span(sp, t):
        for hs, acc in attended_span(1, sp):
            asend[sp, :, hs] = acc.astype(jnp.bfloat16)
        return t

    def own_span(sp, t):
        for hs, acc in attended_span(0, sp):
            both = acc + arecv[sp, :, hs].astype(jnp.float32)
            att[sp, :, hs] = both.astype(jnp.bfloat16)
        return t

    give = remote(asend, arecv, a_s.at[0], a_r.at[0], y_nbr)
    events = 2 * half - 1
    per = -(-ch // 4)

    def sum_step(e, t):
        odd = lax.rem(e, 2)
        m = half - lax.div(e + 1, 2)
        for c in (0, 1):
            d = odd if c == 0 else 1 - odd

            @pl.when(e >= 2)
            def _():
                sum_arrived(d, c, m)

            chunk(d, c, m)
        if events >= 15:
            @pl.when(jnp.logical_and(e >= 1, e <= 4))
            def _():
                lax.fori_loop((e - 1) * per, e * per, nbr_span, 0)

            @pl.when(e == 4)
            def _():
                give.start()

            @pl.when(e == 9)
            def _():
                give.wait_recv()

            @pl.when(jnp.logical_and(e >= 9, e <= 12))
            def _():
                lax.fori_loop((e - 9) * per, (e - 8) * per, own_span, 0)
        return t

    lax.fori_loop(0, events, sum_step, 0)
    if events < 15:
        lax.fori_loop(0, ch, nbr_span, 0)
        give.start()
        give.wait_recv()
        lax.fori_loop(0, ch, own_span, 0)
    out_copy = pltpu.make_async_copy(att, att_out, o_l.at[0])
    out_copy.start()
    finals = []
    for c in (1, 0):
        sum_arrived(0, c, 0)
        sum_arrived(1, c, 0)
        for h in range(heads):
            hs = pl.ds(h * HEAD_DIM, HEAD_DIM)
            o = contribution(c, 0, h) + (rs[0, c, 0, :, :, hs].astype(jnp.float32)
                                         + rs[1, c, 0, :, :, hs].astype(jnp.float32))
            fin[c, :, :, hs] = o.astype(jnp.bfloat16)
        copy = remote(fin.at[c], sg_out.at[c], f_s.at[c], f_r.at[c], sibling)
        copy.start()
        finals.append(copy)

    for d, c in ((0, 0), (1, 1), (0, 1), (1, 0)):
        first(d, c).wait_send()
        steps = half + 1 if d == c else half
        lax.fori_loop(2, steps, lambda k, t: (forward(d, c, k).wait_send(), t)[1], 0)
        lax.fori_loop(1, steps, lambda m, t: (step_on(d, c, m).wait_send(), t)[1], 0)
    for copy in locals_ + swap + [stats, give]:
        copy.wait_send()
    for copy in finals:
        copy.wait_send()
        copy.wait_recv()
    out_copy.wait()


def tables(owner_part, slot_part, count_part, nz):
    packed = jnp.concatenate([owner_part, slot_part, count_part[:, None]], axis=1)
    own = lax.all_gather(packed, "tensor", axis=0, tiled=True)
    size = 2 * nz
    other = lax.ppermute(own, "seq", [(i, (i + nz) % size) for i in range(size)])
    meta = jnp.stack([own, other])
    ch = own.shape[0]
    seq = lax.axis_index("seq")
    y, z = seq // nz, seq % nz
    owner, entry, count = meta[..., 0:2], meta[..., 2:4], meta[..., 4:5]
    j_of = jnp.broadcast_to(jnp.arange(NEIGH)[None, None, :], owner.shape)
    used = (j_of < count) & (owner // nz == y)
    units = ch * NEIGH
    shape = owner.shape
    flat = lambda a: jnp.broadcast_to(a, shape).reshape(2, units)
    owner, entry, used, j_of = flat(owner), flat(entry), flat(used), flat(j_of)
    span = flat(jnp.arange(ch)[None, :, None])
    same = (owner[:, :, None] == owner[:, None, :]) & used[:, None, :]
    earlier = jnp.arange(units)[None, :] < jnp.arange(units)[:, None]
    rank = jnp.sum((same & earlier).astype(jnp.int32), axis=2)
    rel = (owner - z) % nz
    block = jnp.arange(2)[:, None]
    dest = rel * SLOTS + block * 2 + rank
    y_b = jnp.where(block == 0, y, 1 - y)
    lane = y_b * ch + span
    slots = nz * SLOTS
    match = ((dest[None] == jnp.arange(slots)[:, None, None]) & used[None]).astype(jnp.int32)
    total = lambda a: jnp.sum(match * a, axis=(1, 2))
    lane_of = [total((lane - NONE) * (j_of == j)) + NONE for j in range(NEIGH)]
    dest = jnp.where(used, dest, 0)
    parts = [total(span), total(entry), lane_of[0], lane_of[1],
             dest.reshape(-1), (dest // SLOTS).reshape(-1), jnp.where(used, entry, 0).reshape(-1)]
    return jnp.concatenate(parts).astype(jnp.int32)


def per_device(nz, queries, store_kv, out_grad, neighbour_owner, neighbour_slot, neighbour_count):
    rows, width = queries.shape
    heads = width // HEAD_DIM
    ch = rows // SPAN
    half = nz // 2
    entries = store_kv.shape[1] // NLEN
    tab = tables(neighbour_owner, neighbour_slot, neighbour_count, nz)
    bf, f32 = jnp.bfloat16, jnp.float32
    dma = pltpu.SemaphoreType.DMA
    block = (entries, NLEN, width)
    spans = (ch, SPAN, width)
    any_spec = pl.BlockSpec(memory_space=pl.ANY)
    attended, store_grad = pl.pallas_call(
        functools.partial(kernel, nz, ch, heads),
        out_shape=[jax.ShapeDtypeStruct(spans, bf), jax.ShapeDtypeStruct((2,) + block, bf)],
        in_specs=[pl.BlockSpec(memory_space=pltpu.SMEM), any_spec, any_spec, any_spec],
        out_specs=[any_spec, any_spec],
        scratch_shapes=[
            pltpu.VMEM((2, nz) + block, bf),
            pltpu.VMEM(spans, bf), pltpu.VMEM(spans, bf),
            pltpu.VMEM(spans, bf), pltpu.VMEM(spans, bf),
            pltpu.VMEM((nz * SLOTS, SPAN, width), f32),
            pltpu.VMEM((nz * SLOTS, SPAN, width), f32),
            pltpu.VMEM((2, 2, half + 1) + block, bf),
            pltpu.VMEM((2,) + block, bf),
            pltpu.VMEM(spans, bf), pltpu.VMEM(spans, bf), pltpu.VMEM(spans, bf),
            pltpu.VMEM((2, SPAN, 128), f32), pltpu.VMEM((2, SPAN, 128), f32),
            pltpu.VMEM((2, SPAN, 128), f32), pltpu.VMEM((2, SPAN, 128), f32),
            pltpu.VMEM((2, SPAN, 128), f32), pltpu.VMEM((SPAN, 128), f32),
            dma((2, 2, half + 1)), dma((2, 2, half + 1)), dma((2,)), dma((2,)),
            dma((2,)), dma((2,)), dma((2,)), dma((1,)), dma((1,)),
            dma((2, 2, half + 1)), dma((2, 2, half + 1)), dma((1,)), dma((1,)),
            dma((2,)), dma((2,)), dma((1,)),
        ],
        compiler_params=pltpu.CompilerParams(
            collective_id=0, has_side_effects=True, vmem_limit_bytes=60 * 1024 * 1024),
        cost_estimate=pl.CostEstimate(flops=4 * 10 ** 9, bytes_accessed=6 * 10 ** 6,
                                      transcendentals=4 * 10 ** 6),
    )(tab, queries.reshape(spans), store_kv.reshape((2,) + block), out_grad.reshape(spans))
    return attended.reshape(rows, width), store_grad.reshape(store_kv.shape)


def solution(mesh):
    nz = mesh.shape["seq"] // 2
    in_specs = (
        P(("section", "seq"), "tensor"),
        P(None, ("section", "seq"), "tensor"),
        P(("section", "seq"), "tensor"),
        P(("section", "seq", "tensor"), None),
        P(("section", "seq", "tensor"), None),
        P(("section", "seq", "tensor")),
    )
    out_specs = (P(("section", "seq"), "tensor"), P(None, ("section", "seq"), "tensor"))
    return jax.shard_map(
        functools.partial(per_device, nz), mesh=mesh, in_specs=in_specs, out_specs=out_specs,
        check_vma=False)
```

```python
import functools

import jax
import jax.numpy as jnp
from jax import lax
from jax.experimental import pallas as pl
from jax.experimental.pallas import tpu as pltpu
from jax.sharding import PartitionSpec as P

HEAD_DIM = 128
SPAN = 64
NLEN = 128
NEIGH = 2
SLOTS = 4
MESH = pl.DeviceIdType.MESH
DEAD = -1e30
NONE = -100000


def kernel(nz, nt, ch, heads, owner_in, entry_in, count_in, q_in, kv_in, g_in, att_out, sg_out,
           kv, q_own, q_nbr, g_own, g_nbr, pb, dpb, rs, fin, asend, arecv, att,
           lse, gp, st_s, st_r, wts, dlt,
           ag_s, ag_r, loc_s, loc_r, qg_s, qg_r, own_l, stx_s, stx_r,
           rs_s, rs_r, a_s, a_r, f_s, f_r, o_l,
           meta, made, made_u, tab, tab_u, me_s, me_r, t_l):
    half = nz // 2
    stride = 2 * ch
    per_t = ch // nt
    scaling = HEAD_DIM ** (-0.5)
    q_blk, g_blk = (q_own, q_nbr), (g_own, g_nbr)
    sec = lax.axis_index("section")
    seq = lax.axis_index("seq")
    ten = lax.axis_index("tensor")
    y, z = lax.div(seq, nz), lax.rem(seq, nz)
    up, down = lax.rem(z + 1, nz), lax.rem(z + nz - 1, nz)
    z_to = (up, down)

    def dev(s, yy, zz):
        return {"section": s, "seq": yy * nz + zz}

    sibling = dev(1 - sec, y, z)
    y_nbr = dev(sec, 1 - y, z)

    def peer(b, dt):
        return {"seq": (y if b == 0 else 1 - y) * nz + z, "tensor": lax.rem(ten + dt, nt)}

    def remote(src, dst, ssem, rsem, device):
        return pltpu.make_async_remote_copy(
            src_ref=src, dst_ref=dst, send_sem=ssem, recv_sem=rsem,
            device_id=device, device_id_type=MESH)

    barrier = pltpu.get_barrier_semaphore()
    for device in (sibling, y_nbr, dev(sec, y, up), dev(sec, y, down),
                   dev(1 - sec, y, up), dev(1 - sec, y, down)) + tuple(
                       peer(b, dt) for b in (0, 1) for dt in range(1, nt)):
        pl.semaphore_signal(barrier, inc=1, device_id=device, device_id_type=MESH)
    own_q = pltpu.make_async_copy(q_in, q_own, own_l.at[0])
    own_g = pltpu.make_async_copy(g_in, g_own, own_l.at[1])
    own_q.start()
    own_g.start()
    lanes8 = lax.broadcasted_iota(jnp.int32, (8, 128), 1)
    rows8 = lax.broadcasted_iota(jnp.int32, (8, 128), 0)
    mine = jnp.zeros((8, 128), jnp.int32)
    for s in range(per_t):
        for j in range(NEIGH):
            at = lanes8 == (ten * per_t + s) * NEIGH + j
            for row, value in enumerate((owner_in[s, j], entry_in[s, j], count_in[s])):
                mine = jnp.where(jnp.logical_and(at, rows8 == row), value, mine)
    meta[0, ten] = mine
    pl.semaphore_wait(barrier, 6 + 2 * (nt - 1))

    def place(d, k):
        return nz - k if d == 0 else k

    def first(d, c):
        return remote(kv_in.at[c], kv.at[c, place(d, 1)], ag_s.at[d, c, 1], ag_r.at[d, c, 1],
                      dev(1 - sec, y, z_to[d]))

    def forward(d, c, k):
        return remote(kv.at[c, place(d, k - 1)], kv.at[c, place(d, k)], ag_s.at[d, c, k],
                      ag_r.at[d, c, k], dev(sec, y, z_to[d]))

    def arrived(d, c, k):
        here = kv.at[c, place(d, k)]
        remote(here, here, ag_s.at[d, c, k], ag_r.at[d, c, k], dev(sec, y, z_to[d])).wait_recv()

    first(0, 0).start()
    first(1, 1).start()
    first(0, 1).start()
    first(1, 0).start()
    locals_ = [remote(kv_in.at[c], kv.at[c, 0], loc_s.at[c], loc_r.at[c], sibling) for c in (0, 1)]
    for copy in locals_:
        copy.start()
    maps = [remote(meta.at[0, ten], meta.at[b, ten], me_s.at[b, dt], me_r.at[b, dt],
                   peer(b, dt)) for dt in range(nt) for b in (0, 1) if b + dt > 0]
    for copy in maps:
        copy.start()
    swap = [remote(q_in, q_nbr, qg_s.at[0], qg_r.at[0], y_nbr),
            remote(g_in, g_nbr, qg_s.at[1], qg_r.at[1], y_nbr)]
    for copy in swap:
        copy.start()

    lse[...] = jnp.full_like(lse, DEAD)
    gp[...] = jnp.zeros_like(gp)
    for d, c, m in ((0, 0, half), (1, 1, half), (0, 1, half - 1), (1, 0, half - 1)):
        rs[d, c, m] = jnp.zeros(rs.shape[3:], rs.dtype)
    lanes = lax.broadcasted_iota(jnp.int32, (SPAN, 128), 1)

    def build_tables():
        for dt in range(nt):
            for b in (0, 1):
                if b + dt > 0:
                    here = meta.at[b, lax.rem(ten + nt - dt, nt)]
                    remote(here, here, me_s.at[b, dt], me_r.at[b, dt], peer(b, dt)).wait_recv()
        unit = lax.broadcasted_iota(jnp.int32, (nz, 128), 1)
        row = lax.broadcasted_iota(jnp.int32, (nz, 128), 0)
        made_all = jnp.zeros((nz, 128), jnp.int32)
        unit_all = jnp.zeros((8, 128), jnp.int32)
        for b in (0, 1):
            whole = meta[b, 0]
            for t in range(1, nt):
                whole = whole + meta[b, t]
            spread = lambda i: jnp.broadcast_to(whole[i:i + 1], (nz, 128))
            owner, entry, count = spread(0), spread(1), spread(2)
            j_of = lax.bitwise_and(unit, 1)
            span = lax.shift_right_logical(unit, 1)
            col = owner - y * nz
            used = ((unit < ch * NEIGH) & (j_of < count)) & ((col >= 0) & (col < nz))
            rel = jnp.where(col < z, col - z + nz, col - z)
            mine = jnp.logical_and(used, rel == row)
            u0 = jnp.min(jnp.where(mine, unit, 1000), axis=1, keepdims=True)
            u1 = jnp.max(jnp.where(mine, unit, -1), axis=1, keepdims=True)
            u1 = jnp.where(u1 == u0, -1, u1)
            lane = (y if b == 0 else 1 - y) * ch + span
            for r, u in ((0, u0), (1, u1)):
                at = unit == u
                get = lambda v: jnp.sum(jnp.where(at, v, 0), axis=1, keepdims=True)
                values = (get(span), get(entry)) + tuple(
                    get(jnp.where(j_of == j, lane - NONE, 0)) + NONE for j in range(NEIGH))
                for i, value in enumerate(values):
                    made_all = jnp.where(unit == i * SLOTS + b * 2 + r, value, made_all)
            rank = jnp.sum(jnp.where(jnp.logical_and(mine, unit != u0), 1, 0), axis=0, keepdims=True)
            use1, rel1, entry1 = used[0:1], rel[0:1], entry[0:1]
            for i, value in enumerate((rel1, b * 2 + rank, entry1)):
                value = jnp.broadcast_to(jnp.where(use1, value, 0), (8, 128))
                unit_all = jnp.where(rows8 == b * 3 + i, value, unit_all)
        made[...] = made_all
        made_u[...] = unit_all
        copies = [pltpu.make_async_copy(made, tab, t_l.at[0]),
                  pltpu.make_async_copy(made_u, tab_u, t_l.at[1])]
        for copy in copies:
            copy.start()
        for copy in copies:
            copy.wait()

    def pick(three, es):
        return jnp.where(es == 0, three[0], jnp.where(es == 1, three[1], three[2]))

    def fwd_item(n, b):
        idx = jnp.where(lax.rem(n, 2) == 1, nz - lax.div(n + 1, 2), lax.div(n, 2))
        for r in (0, 1):
            slot = b * 2 + r
            sl = idx * SLOTS + slot
            sp, es = tab[idx, slot], tab[idx, SLOTS + slot]
            l_of = (tab[idx, 2 * SLOTS + slot], tab[idx, 3 * SLOTS + slot])
            stat_l, stat_g = [], []
            for h in range(heads):
                hs = pl.ds(h * HEAD_DIM, HEAD_DIM)
                qv = q_blk[b][sp, :, hs]
                gv = g_blk[b][sp, :, hs]
                ks = pick([kv[0, idx, e, :, hs] for e in range(3)], es)
                vs = pick([kv[1, idx, e, :, hs] for e in range(3)], es)
                s = lax.dot_general(qv, ks, (((1,), (1,)), ((), ())),
                                    preferred_element_type=jnp.float32) * scaling
                dp = lax.dot_general(gv, vs, (((1,), (1,)), ((), ())),
                                     preferred_element_type=jnp.float32)
                top = jnp.max(s, axis=1, keepdims=True)
                p = jnp.exp(s - top)
                tot = jnp.sum(p, axis=1, keepdims=True)
                p = p * (1.0 / tot)
                pb[sl, :, hs] = p
                dpb[sl, :, hs] = dp
                stat_l.append(top + jnp.log(tot))
                stat_g.append(jnp.sum(p * dp, axis=1, keepdims=True))
            for j in range(NEIGH):
                a, g2 = lse[j], gp[j]
                for h in range(heads):
                    hit = lanes == l_of[j] + h * stride
                    a = jnp.where(hit, stat_l[h], a)
                    g2 = jnp.where(hit, stat_g[h], g2)
                lse[j] = a
                gp[j] = g2

    def items(lo, hi, b):
        lax.fori_loop(lo, hi, lambda n, t: (fwd_item(n, b), t)[1], 0)

    own_q.wait()
    own_g.wait()
    for copy in locals_:
        copy.wait_recv()
    build_tables()
    lag = min(4, half)

    def nbr_done(k):
        return jnp.minimum(jnp.maximum((k + 1 - lag) * 4, 0), 2 * half - 3)

    def gather_step(k, t):
        for d, c in ((0, 0), (1, 1)):
            arrived(d, c, k)
            forward(d, c, k + 1).start()
        items(jnp.maximum(2 * k - 3, 0), 2 * k - 1, 0)
        for d, c in ((0, 1), (1, 0)):
            arrived(d, c, k)

            @pl.when(k + 1 < half)
            def _():
                forward(d, c, k + 1).start()

        @pl.when(k == lag)
        def _():
            for copy in swap:
                copy.wait_recv()

        items(nbr_done(k - 1), nbr_done(k), 1)
        return t

    lax.fori_loop(1, half, gather_step, 0)
    if half <= lag:
        for copy in swap:
            copy.wait_recv()
    items(2 * half - 3, 2 * half - 1, 0)
    items(nbr_done(half - 1), 2 * half - 1, 1)
    arrived(0, 0, half)
    arrived(1, 1, half)
    fwd_item(2 * half - 1, 0)
    fwd_item(2 * half - 1, 1)

    a0, a1 = lse[0], lse[1]
    top = jnp.maximum(a0, a1)
    lc = top + jnp.log(jnp.exp(a0 - top) + jnp.exp(a1 - top))
    gc = jnp.exp(a0 - lc) * gp[0] + jnp.exp(a1 - lc) * gp[1]
    st_s[0] = lc
    st_s[1] = gc
    stats = remote(st_s, st_r, stx_s.at[0], stx_r.at[0], y_nbr)
    stats.start()
    stats.wait_recv()
    lo_, go_ = st_r[0], st_r[1]
    top = jnp.maximum(lc, lo_)
    total = top + jnp.log(jnp.exp(lc - top) + jnp.exp(lo_ - top))
    dlt[...] = jnp.exp(lc - total) * gc + jnp.exp(lo_ - total) * go_
    wts[0] = jnp.exp(a0 - total)
    wts[1] = jnp.exp(a1 - total)

    def column(values, lane):
        return jnp.sum(jnp.where(lanes == lane, values, 0.0), axis=1, keepdims=True)

    def contribution(c, idx, h):
        hs = pl.ds(h * HEAD_DIM, HEAD_DIM)
        left, right = [], []
        for slot in range(SLOTS):
            b = slot // 2
            sl = idx * SLOTS + slot
            sp, es = tab[idx, slot], tab[idx, SLOTS + slot]
            l0 = tab[idx, 2 * SLOTS + slot] + h * stride
            l1 = tab[idx, 3 * SLOTS + slot] + h * stride
            w = jnp.where(lanes == l0, wts[0], 0.0) + jnp.where(lanes == l1, wts[1], 0.0)
            p = pb[sl, :, hs] * jnp.sum(w, axis=1, keepdims=True)
            if c == 0:
                p = p * (dpb[sl, :, hs] - column(dlt[...], jnp.maximum(l0, l1)))
                right.append(q_blk[b][sp, :, hs])
            else:
                right.append(g_blk[b][sp, :, hs])
            x = p.astype(jnp.bfloat16)
            zero = jnp.zeros_like(x)
            left.append(jnp.concatenate([jnp.where(es == e, x, zero) for e in range(3)], axis=1))
        out = lax.dot_general(jnp.concatenate(left, axis=0), jnp.concatenate(right, axis=0),
                              (((0,), (0,)), ((), ())), preferred_element_type=jnp.float32)
        if c == 0:
            out = out * scaling
        return out.reshape(3, NLEN, HEAD_DIM)

    def step_on(d, c, m):
        zz = lax.rem(z + 1 + d * (nz - 2), nz)
        return remote(rs.at[d, c, m], rs.at[d, c, m - 1], rs_s.at[d, c, m - 1],
                      rs_r.at[d, c, m - 1], dev(sec, y, zz))

    def sum_arrived(d, c, m):
        here = rs.at[d, c, m]
        remote(here, here, rs_s.at[d, c, m], rs_r.at[d, c, m], y_nbr).wait_recv()

    def chunk(d, c, m):
        idx = jnp.where(d == 0, m, nz - m)
        for h in range(heads):
            hs = pl.ds(h * HEAD_DIM, HEAD_DIM)
            o = contribution(c, idx, h) + rs[d, c, m, :, :, hs].astype(jnp.float32)
            rs[d, c, m, :, :, hs] = o.astype(jnp.bfloat16)
        step_on(d, c, m).start()

    def attended_span(b, sp):
        y_b = y if b == 0 else 1 - y
        outs = []
        for h in range(heads):
            hs = pl.ds(h * HEAD_DIM, HEAD_DIM)
            acc = jnp.zeros((SPAN, HEAD_DIM), jnp.float32)
            for j in range(NEIGH):
                at = sp * NEIGH + j
                idx = tab_u[b * 3, at]
                sl = idx * SLOTS + tab_u[b * 3 + 1, at]
                es = tab_u[b * 3 + 2, at]
                w = column(wts[j], y_b * ch + sp + h * stride)
                p = (pb[sl, :, hs] * w).astype(jnp.bfloat16)
                acc += jnp.dot(p, kv[1, idx, es, :, hs], preferred_element_type=jnp.float32)
            outs.append((hs, acc))
        return outs

    def nbr_span(sp, t):
        for hs, acc in attended_span(1, sp):
            asend[sp, :, hs] = acc.astype(jnp.bfloat16)
        return t

    def own_span(sp, t):
        for hs, acc in attended_span(0, sp):
            both = acc + arecv[sp, :, hs].astype(jnp.float32)
            att[sp, :, hs] = both.astype(jnp.bfloat16)
        return t

    give = remote(asend, arecv, a_s.at[0], a_r.at[0], y_nbr)
    events = 2 * half - 1
    per = -(-ch // 4)

    def sum_step(e, t):
        odd = lax.rem(e, 2)
        m = half - lax.div(e + 1, 2)
        for c in (0, 1):
            d = odd if c == 0 else 1 - odd

            @pl.when(e >= 2)
            def _():
                sum_arrived(d, c, m)

            chunk(d, c, m)
        if events >= 15:
            @pl.when(jnp.logical_and(e >= 1, e <= 4))
            def _():
                lax.fori_loop((e - 1) * per, e * per, nbr_span, 0)

            @pl.when(e == 4)
            def _():
                give.start()

            @pl.when(e == 9)
            def _():
                give.wait_recv()

            @pl.when(jnp.logical_and(e >= 9, e <= 12))
            def _():
                lax.fori_loop((e - 9) * per, (e - 8) * per, own_span, 0)
        return t

    lax.fori_loop(0, events, sum_step, 0)
    if events < 15:
        lax.fori_loop(0, ch, nbr_span, 0)
        give.start()
        give.wait_recv()
        lax.fori_loop(0, ch, own_span, 0)
    out_copy = pltpu.make_async_copy(att, att_out, o_l.at[0])
    out_copy.start()
    finals = []
    for c in (1, 0):
        sum_arrived(0, c, 0)
        sum_arrived(1, c, 0)
        for h in range(heads):
            hs = pl.ds(h * HEAD_DIM, HEAD_DIM)
            o = contribution(c, 0, h) + (rs[0, c, 0, :, :, hs].astype(jnp.float32)
                                         + rs[1, c, 0, :, :, hs].astype(jnp.float32))
            fin[c, :, :, hs] = o.astype(jnp.bfloat16)
        copy = remote(fin.at[c], sg_out.at[c], f_s.at[c], f_r.at[c], sibling)
        copy.start()
        finals.append(copy)

    for d, c in ((0, 0), (1, 1), (0, 1), (1, 0)):
        first(d, c).wait_send()
        steps = half + 1 if d == c else half
        lax.fori_loop(2, steps, lambda k, t: (forward(d, c, k).wait_send(), t)[1], 0)
        lax.fori_loop(1, steps, lambda m, t: (step_on(d, c, m).wait_send(), t)[1], 0)
    for copy in locals_ + swap + maps + [stats, give]:
        copy.wait_send()
    for copy in finals:
        copy.wait_send()
        copy.wait_recv()
    out_copy.wait()


def per_device(nz, queries, store_kv, out_grad, neighbour_owner, neighbour_slot, neighbour_count):
    rows, width = queries.shape
    heads = width // HEAD_DIM
    ch = rows // SPAN
    half = nz // 2
    entries = store_kv.shape[1] // NLEN
    nt = lax.axis_size("tensor")
    bf, f32 = jnp.bfloat16, jnp.float32
    dma = pltpu.SemaphoreType.DMA
    block = (entries, NLEN, width)
    spans = (ch, SPAN, width)
    any_spec = pl.BlockSpec(memory_space=pl.ANY)
    attended, store_grad = pl.pallas_call(
        functools.partial(kernel, nz, nt, ch, heads),
        out_shape=[jax.ShapeDtypeStruct(spans, bf), jax.ShapeDtypeStruct((2,) + block, bf)],
        in_specs=[pl.BlockSpec(memory_space=pltpu.SMEM)] * 3 + [any_spec, any_spec, any_spec],
        out_specs=[any_spec, any_spec],
        scratch_shapes=[
            pltpu.VMEM((2, nz) + block, bf),
            pltpu.VMEM(spans, bf), pltpu.VMEM(spans, bf),
            pltpu.VMEM(spans, bf), pltpu.VMEM(spans, bf),
            pltpu.VMEM((nz * SLOTS, SPAN, width), f32),
            pltpu.VMEM((nz * SLOTS, SPAN, width), f32),
            pltpu.VMEM((2, 2, half + 1) + block, bf),
            pltpu.VMEM((2,) + block, bf),
            pltpu.VMEM(spans, bf), pltpu.VMEM(spans, bf), pltpu.VMEM(spans, bf),
            pltpu.VMEM((2, SPAN, 128), f32), pltpu.VMEM((2, SPAN, 128), f32),
            pltpu.VMEM((2, SPAN, 128), f32), pltpu.VMEM((2, SPAN, 128), f32),
            pltpu.VMEM((2, SPAN, 128), f32), pltpu.VMEM((SPAN, 128), f32),
            dma((2, 2, half + 1)), dma((2, 2, half + 1)), dma((2,)), dma((2,)),
            dma((2,)), dma((2,)), dma((2,)), dma((1,)), dma((1,)),
            dma((2, 2, half + 1)), dma((2, 2, half + 1)), dma((1,)), dma((1,)),
            dma((2,)), dma((2,)), dma((1,)),
            pltpu.VMEM((2, nt, 8, 128), jnp.int32), pltpu.VMEM((nz, 128), jnp.int32),
            pltpu.VMEM((8, 128), jnp.int32), pltpu.SMEM((nz, 128), jnp.int32),
            pltpu.SMEM((8, 128), jnp.int32), dma((2, nt)), dma((2, nt)), dma((2,)),
        ],
        compiler_params=pltpu.CompilerParams(
            collective_id=0, has_side_effects=True, vmem_limit_bytes=60 * 1024 * 1024),
        cost_estimate=pl.CostEstimate(flops=4 * 10 ** 9, bytes_accessed=6 * 10 ** 6,
                                      transcendentals=4 * 10 ** 6),
    )(neighbour_owner, neighbour_slot, neighbour_count, queries.reshape(spans), store_kv.reshape((2,) + block), out_grad.reshape(spans))
    return attended.reshape(rows, width), store_grad.reshape(store_kv.shape)


def solution(mesh):
    nz = mesh.shape["seq"] // 2
    in_specs = (
        P(("section", "seq"), "tensor"),
        P(None, ("section", "seq"), "tensor"),
        P(("section", "seq"), "tensor"),
        P(("section", "seq", "tensor"), None),
        P(("section", "seq", "tensor"), None),
        P(("section", "seq", "tensor")),
    )
    out_specs = (P(("section", "seq"), "tensor"), P(None, ("section", "seq"), "tensor"))
    return jax.shard_map(
        functools.partial(per_device, nz), mesh=mesh, in_specs=in_specs, out_specs=out_specs,
        check_vma=False)
```

```python
import functools

import jax
import jax.numpy as jnp
from jax import lax
from jax.experimental import pallas as pl
from jax.experimental.pallas import tpu as pltpu
from jax.sharding import PartitionSpec as P

HEAD_DIM = 128
SPAN = 64
NLEN = 128
NEIGH = 2
SLOTS = 4
MESH = pl.DeviceIdType.MESH
DEAD = -1e30
NONE = -100000


def kernel(nz, nt, ch, heads, owner_in, entry_in, count_in, q_in, kv_in, g_in, att_out, sg_out,
           kv, q_own, q_nbr, g_own, g_nbr, pb, dpb, rs, cbuf, fin, asend, arecv, att,
           lse, gp, st_s, st_r, wts, dlt,
           ag_s, ag_r, loc_s, loc_r, qg_s, qg_r, own_l, stx_s, stx_r,
           rs_s, rs_r, a_s, a_r, f_s, f_r, o_l,
           meta, made, made_u, tab, tab_u, me_s, me_r, t_l):
    half = nz // 2
    stride = 2 * ch
    per_t = ch // nt
    scaling = HEAD_DIM ** (-0.5)
    q_blk, g_blk = (q_own, q_nbr), (g_own, g_nbr)
    sec = lax.axis_index("section")
    seq = lax.axis_index("seq")
    ten = lax.axis_index("tensor")
    y, z = lax.div(seq, nz), lax.rem(seq, nz)
    up, down = lax.rem(z + 1, nz), lax.rem(z + nz - 1, nz)
    z_to = (up, down)

    def dev(s, yy, zz):
        return {"section": s, "seq": yy * nz + zz}

    sibling = dev(1 - sec, y, z)
    y_nbr = dev(sec, 1 - y, z)

    def peer(b, dt):
        return {"seq": (y if b == 0 else 1 - y) * nz + z, "tensor": lax.rem(ten + dt, nt)}

    def remote(src, dst, ssem, rsem, device):
        return pltpu.make_async_remote_copy(
            src_ref=src, dst_ref=dst, send_sem=ssem, recv_sem=rsem,
            device_id=device, device_id_type=MESH)

    barrier = pltpu.get_barrier_semaphore()
    for device in (sibling, y_nbr, dev(sec, y, up), dev(sec, y, down),
                   dev(1 - sec, y, up), dev(1 - sec, y, down)) + tuple(
                       peer(b, dt) for b in (0, 1) for dt in range(1, nt)):
        pl.semaphore_signal(barrier, inc=1, device_id=device, device_id_type=MESH)
    own_q = pltpu.make_async_copy(q_in, q_own, own_l.at[0])
    own_g = pltpu.make_async_copy(g_in, g_own, own_l.at[1])
    own_q.start()
    own_g.start()
    lanes8 = lax.broadcasted_iota(jnp.int32, (8, 128), 1)
    rows8 = lax.broadcasted_iota(jnp.int32, (8, 128), 0)
    mine = jnp.zeros((8, 128), jnp.int32)
    for s in range(per_t):
        for j in range(NEIGH):
            at = lanes8 == (ten * per_t + s) * NEIGH + j
            for row, value in enumerate((owner_in[s, j], entry_in[s, j], count_in[s])):
                mine = jnp.where(jnp.logical_and(at, rows8 == row), value, mine)
    meta[0, ten] = mine
    pl.semaphore_wait(barrier, 6 + 2 * (nt - 1))

    def place(d, k):
        return nz - k if d == 0 else k

    def far(c, e):
        return 0 if e < 2 - c else 1

    def first(d, c, e):
        return remote(kv_in.at[c, e], kv.at[c, place(d, 1), e], ag_s.at[d, c, 1, e],
                      ag_r.at[d, c, 1, e], dev(1 - sec, y, z_to[d]))

    def forward(d, c, k, e):
        return remote(kv.at[c, place(d, k - 1), e], kv.at[c, place(d, k), e], ag_s.at[d, c, k, e],
                      ag_r.at[d, c, k, e], dev(sec, y, z_to[d]))

    def arrived(d, c, k, e):
        here = kv.at[c, place(d, k), e]
        remote(here, here, ag_s.at[d, c, k, e], ag_r.at[d, c, k, e],
               dev(sec, y, z_to[d])).wait_recv()

    def pass_on(c, k, e):
        for d in (0, 1):
            arrived(d, c, k, e)
            if not isinstance(k, int) or k != half - 1 or far(c, e) == d:
                forward(d, c, k + 1, e).start()

    def start_gather():
        for e in range(3):
            for c in (0, 1):
                for d in (0, 1):
                    first(d, c, e).start()

    def end_gather(c):
        for e in range(3):
            arrived(far(c, e), c, half, e)

    start_gather()
    locals_ = [remote(kv_in.at[c], kv.at[c, 0], loc_s.at[c], loc_r.at[c], sibling) for c in (0, 1)]
    for copy in locals_:
        copy.start()
    maps = [remote(meta.at[0, ten], meta.at[b, ten], me_s.at[b, dt], me_r.at[b, dt],
                   peer(b, dt)) for dt in range(nt) for b in (0, 1) if b + dt > 0]
    for copy in maps:
        copy.start()
    swap = [remote(q_in, q_nbr, qg_s.at[0], qg_r.at[0], y_nbr),
            remote(g_in, g_nbr, qg_s.at[1], qg_r.at[1], y_nbr)]
    for copy in swap:
        copy.start()

    lse[...] = jnp.full_like(lse, DEAD)
    gp[...] = jnp.zeros_like(gp)
    lanes = lax.broadcasted_iota(jnp.int32, (SPAN, 128), 1)

    def build_tables():
        for dt in range(nt):
            for b in (0, 1):
                if b + dt > 0:
                    here = meta.at[b, lax.rem(ten + nt - dt, nt)]
                    remote(here, here, me_s.at[b, dt], me_r.at[b, dt], peer(b, dt)).wait_recv()
        unit = lax.broadcasted_iota(jnp.int32, (nz, 128), 1)
        row = lax.broadcasted_iota(jnp.int32, (nz, 128), 0)
        made_all = jnp.zeros((nz, 128), jnp.int32)
        unit_all = jnp.zeros((8, 128), jnp.int32)
        for b in (0, 1):
            whole = meta[b, 0]
            for t in range(1, nt):
                whole = whole + meta[b, t]
            spread = lambda i: jnp.broadcast_to(whole[i:i + 1], (nz, 128))
            owner, entry, count = spread(0), spread(1), spread(2)
            j_of = lax.bitwise_and(unit, 1)
            span = lax.shift_right_logical(unit, 1)
            col = owner - y * nz
            used = ((unit < ch * NEIGH) & (j_of < count)) & ((col >= 0) & (col < nz))
            rel = jnp.where(col < z, col - z + nz, col - z)
            mine = jnp.logical_and(used, rel == row)
            u0 = jnp.min(jnp.where(mine, unit, 1000), axis=1, keepdims=True)
            u1 = jnp.max(jnp.where(mine, unit, -1), axis=1, keepdims=True)
            u1 = jnp.where(u1 == u0, -1, u1)
            lane = (y if b == 0 else 1 - y) * ch + span
            for r, u in ((0, u0), (1, u1)):
                at = unit == u
                get = lambda v: jnp.sum(jnp.where(at, v, 0), axis=1, keepdims=True)
                values = (get(span), get(entry)) + tuple(
                    get(jnp.where(j_of == j, lane - NONE, 0)) + NONE for j in range(NEIGH))
                for i, value in enumerate(values):
                    made_all = jnp.where(unit == i * SLOTS + b * 2 + r, value, made_all)
            rank = jnp.sum(jnp.where(jnp.logical_and(mine, unit != u0), 1, 0), axis=0, keepdims=True)
            use1, rel1, entry1 = used[0:1], rel[0:1], entry[0:1]
            for i, value in enumerate((rel1, b * 2 + rank, entry1)):
                value = jnp.broadcast_to(jnp.where(use1, value, 0), (8, 128))
                unit_all = jnp.where(rows8 == b * 3 + i, value, unit_all)
        made[...] = made_all
        made_u[...] = unit_all
        copies = [pltpu.make_async_copy(made, tab, t_l.at[0]),
                  pltpu.make_async_copy(made_u, tab_u, t_l.at[1])]
        for copy in copies:
            copy.start()
        for copy in copies:
            copy.wait()

    def pick(three, es):
        return jnp.where(es == 0, three[0], jnp.where(es == 1, three[1], three[2]))

    def place_of(n):
        return jnp.where(lax.rem(n, 2) == 1, nz - lax.div(n + 1, 2), lax.div(n, 2))

    def insert(ref, idx, slot, columns):
        for j in range(NEIGH):
            lane = tab[idx, (2 + j) * SLOTS + slot]
            a = ref[j]
            for h in range(heads):
                a = jnp.where(lanes == lane + h * stride, columns[h], a)
            ref[j] = a

    def score_item(n, b):
        idx = place_of(n)
        for r in (0, 1):
            slot = b * 2 + r
            sl = idx * SLOTS + slot
            sp, es = tab[idx, slot], tab[idx, SLOTS + slot]
            columns = []
            for h in range(heads):
                hs = pl.ds(h * HEAD_DIM, HEAD_DIM)
                ks = pick([kv[0, idx, e, :, hs] for e in range(3)], es)
                s = lax.dot_general(q_blk[b][sp, :, hs], ks, (((1,), (1,)), ((), ())),
                                    preferred_element_type=jnp.float32) * scaling
                top = jnp.max(s, axis=1, keepdims=True)
                p = jnp.exp(s - top)
                tot = jnp.sum(p, axis=1, keepdims=True)
                pb[sl, :, hs] = p * (1.0 / tot)
                columns.append(top + jnp.log(tot))
            insert(lse, idx, slot, columns)

    def grad_item(n, b):
        idx = place_of(n)
        for r in (0, 1):
            slot = b * 2 + r
            sl = idx * SLOTS + slot
            sp, es = tab[idx, slot], tab[idx, SLOTS + slot]
            columns = []
            for h in range(heads):
                hs = pl.ds(h * HEAD_DIM, HEAD_DIM)
                vs = pick([kv[1, idx, e, :, hs] for e in range(3)], es)
                dp = lax.dot_general(g_blk[b][sp, :, hs], vs, (((1,), (1,)), ((), ())),
                                     preferred_element_type=jnp.float32)
                dpb[sl, :, hs] = dp
                columns.append(jnp.sum(pb[sl, :, hs] * dp, axis=1, keepdims=True))
            insert(gp, idx, slot, columns)

    def items(work, lo, hi, b):
        lax.fori_loop(lo, hi, lambda n, t: (work(n, b), t)[1], 0)

    own_q.wait()
    own_g.wait()
    for copy in locals_:
        copy.wait_recv()
    build_tables()
    lag = 4

    def done(k):
        return jnp.maximum((k + 1 - lag) * 4, 0)

    def upto(step):
        return max(2 * step + 1, 0)

    def gather_step(k, t):
        pass_on(0, k, 0)
        items(score_item, jnp.maximum(2 * k - 3, 0), 2 * k - 1, 0)
        pass_on(1, k, 0)

        @pl.when(k == lag)
        def _():
            for copy in swap:
                copy.wait_recv()

        lo, hi = done(k - 1), done(k)
        mid = jnp.minimum(lo + 2, hi)
        items(score_item, lo, mid, 1)
        pass_on(0, k, 1)
        items(score_item, mid, hi, 1)
        pass_on(1, k, 1)
        items(grad_item, lo, hi, 0)
        pass_on(0, k, 2)
        items(grad_item, lo, hi, 1)
        pass_on(1, k, 2)
        return t

    both = half - 3
    lax.fori_loop(1, both + 1, gather_step, 0)
    if both < lag:
        for copy in swap:
            copy.wait_recv()
    own_at = upto(both - 1)
    nbr_at = max((both + 1 - lag) * 4, 0)
    if half > 2:
        for e in range(3):
            pass_on(0, half - 2, e)
        pass_on(1, half - 2, 0)
    items(score_item, own_at, upto(both), 0)
    items(score_item, nbr_at, upto(both), 1)
    for e in range(3):
        pass_on(0, half - 1, e)
    if half > 2:
        pass_on(1, half - 2, 1)
        pass_on(1, half - 2, 2)
    for b in (0, 1):
        items(score_item, upto(both), upto(half - 1), b)
    for b in (0, 1):
        items(grad_item, nbr_at, upto(half - 2), b)
    end_gather(0)
    for b in (0, 1):
        items(score_item, upto(half - 1), 2 * half, b)

    def exchange(i, value):
        st_s[i] = value
        copy = remote(st_s.at[i], st_r.at[i], stx_s.at[i], stx_r.at[i], y_nbr)
        copy.start()
        copy.wait_recv()
        return copy

    a0, a1 = lse[0], lse[1]
    top = jnp.maximum(a0, a1)
    lc = top + jnp.log(jnp.exp(a0 - top) + jnp.exp(a1 - top))
    stats = [exchange(0, lc)]
    lo_ = st_r[0]
    top = jnp.maximum(lc, lo_)
    total = top + jnp.log(jnp.exp(lc - top) + jnp.exp(lo_ - top))
    wts[0] = jnp.exp(a0 - total)
    wts[1] = jnp.exp(a1 - total)
    for e in range(3):
        pass_on(1, half - 1, e)

    def column(values, lane):
        return jnp.sum(jnp.where(lanes == lane, values, 0.0), axis=1, keepdims=True)

    def contribution(c, idx, h):
        hs = pl.ds(h * HEAD_DIM, HEAD_DIM)
        left, right = [], []
        for slot in range(SLOTS):
            b = slot // 2
            sl = idx * SLOTS + slot
            sp, es = tab[idx, slot], tab[idx, SLOTS + slot]
            l0 = tab[idx, 2 * SLOTS + slot] + h * stride
            l1 = tab[idx, 3 * SLOTS + slot] + h * stride
            w = jnp.where(lanes == l0, wts[0], 0.0) + jnp.where(lanes == l1, wts[1], 0.0)
            p = pb[sl, :, hs] * jnp.sum(w, axis=1, keepdims=True)
            if c == 0:
                p = p * (dpb[sl, :, hs] - column(dlt[...], jnp.maximum(l0, l1)))
                right.append(q_blk[b][sp, :, hs])
            else:
                right.append(g_blk[b][sp, :, hs])
            x = p.astype(jnp.bfloat16)
            zero = jnp.zeros_like(x)
            left.append(jnp.concatenate([jnp.where(es == e, x, zero) for e in range(3)], axis=1))
        out = lax.dot_general(jnp.concatenate(left, axis=0), jnp.concatenate(right, axis=0),
                              (((0,), (0,)), ((), ())), preferred_element_type=jnp.float32)
        if c == 0:
            out = out * scaling
        return out.reshape(3, NLEN, HEAD_DIM)

    def contribute(c, idx, into):
        for h in range(heads):
            cbuf[c, into, :, :, pl.ds(h * HEAD_DIM, HEAD_DIM)] = contribution(c, idx, h)

    def step_on(d, c, m, e):
        return remote(rs.at[d, c, m, e], rs.at[d, c, m - 1, e], rs_s.at[d, c, m - 1, e],
                      rs_r.at[d, c, m - 1, e], dev(sec, y, z_to[d]))

    def sum_arrived(d, c, m, e):
        here = rs.at[d, c, m, e]
        remote(here, here, rs_s.at[d, c, m, e], rs_r.at[d, c, m, e], y_nbr).wait_recv()

    def contribute_both(c, m):
        lax.fori_loop(0, 2, lambda d, t: (contribute(c, jnp.where(d == 0, m, nz - m), d), t)[1], 0)

    def start_sums(c):
        contribute(c, half, 0)
        for e in range(3):
            d = far(c, e)
            rs[d, c, half, e] = cbuf[c, 0, e].astype(jnp.bfloat16)
            step_on(d, c, half, e).start()
        contribute_both(c, half - 1)
        for e in range(3):
            d = 1 - far(c, e)
            rs[d, c, half - 1, e] = cbuf[c, d, e].astype(jnp.bfloat16)
            step_on(d, c, half - 1, e).start()

    def add_on(c, d, m, e):
        sum_arrived(d, c, m, e)
        o = cbuf[c, d, e] + rs[d, c, m, e].astype(jnp.float32)
        rs[d, c, m, e] = o.astype(jnp.bfloat16)
        step_on(d, c, m, e).start()

    def last_sum(c, e):
        sum_arrived(0, c, 0, e)
        sum_arrived(1, c, 0, e)
        o = cbuf[c, 0, e] + (rs[0, c, 0, e].astype(jnp.float32) + rs[1, c, 0, e].astype(jnp.float32))
        fin[c, e] = o.astype(jnp.bfloat16)
        give_back(c, e).start()

    def give_back(c, e):
        return remote(fin.at[c, e], sg_out.at[c, e], f_s.at[c, e], f_r.at[c, e], sibling)

    def attended_span(b, sp):
        y_b = y if b == 0 else 1 - y
        outs = []
        for h in range(heads):
            hs = pl.ds(h * HEAD_DIM, HEAD_DIM)
            acc = jnp.zeros((SPAN, HEAD_DIM), jnp.float32)
            for j in range(NEIGH):
                at = sp * NEIGH + j
                idx = tab_u[b * 3, at]
                sl = idx * SLOTS + tab_u[b * 3 + 1, at]
                es = tab_u[b * 3 + 2, at]
                w = column(wts[j], y_b * ch + sp + h * stride)
                p = (pb[sl, :, hs] * w).astype(jnp.bfloat16)
                acc += jnp.dot(p, kv[1, idx, es, :, hs], preferred_element_type=jnp.float32)
            outs.append((hs, acc))
        return outs

    def nbr_span(sp, t):
        for hs, acc in attended_span(1, sp):
            asend[sp, :, hs] = acc.astype(jnp.bfloat16)
        return t

    def own_span(sp, t):
        for hs, acc in attended_span(0, sp):
            both = acc + arecv[sp, :, hs].astype(jnp.float32)
            att[sp, :, hs] = both.astype(jnp.bfloat16)
        return t

    give = remote(asend, arecv, a_s.at[0], a_r.at[0], y_nbr)
    out_copy = pltpu.make_async_copy(att, att_out, o_l.at[0])

    start_sums(1)
    end_gather(1)
    for b in (0, 1):
        items(grad_item, upto(half - 2), 2 * half, b)
    gc = wts[0] * gp[0] + wts[1] * gp[1]
    stats.append(exchange(1, gc))
    dlt[...] = gc + st_r[1]
    start_sums(0)
    for e in range(3):
        for c in (1, 0):
            add_on(c, far(c, e), half - 1, e)

    def spans(k):
        if half < 8:
            return

        @pl.when(k <= 3)
        def _():
            lax.fori_loop((k - 2) * (ch // 2), (k - 1) * (ch // 2), nbr_span, 0)

        @pl.when(k == 3)
        def _():
            give.start()

        @pl.when(k == 6)
        def _():
            give.wait_recv()

        @pl.when(jnp.logical_and(k >= 6, k <= 7))
        def _():
            lax.fori_loop((k - 6) * (ch // 2), (k - 5) * (ch // 2), own_span, 0)

        @pl.when(k == 7)
        def _():
            out_copy.start()

    def sum_step(k, t):
        m = half - k
        contribute_both(1, m)
        contribute_both(0, m)
        for e in range(3):
            for c in (1, 0):
                for d in (0, 1):
                    add_on(c, d, m, e)
        spans(k)
        return t

    lax.fori_loop(2, half, sum_step, 0)
    if half < 8:
        lax.fori_loop(0, ch, nbr_span, 0)
        give.start()
        give.wait_recv()
        lax.fori_loop(0, ch, own_span, 0)
        out_copy.start()
    contribute(1, 0, 0)
    contribute(0, 0, 0)
    for e in range(3):
        for c in (1, 0):
            last_sum(c, e)

    for c in (0, 1):
        for d in (0, 1):
            for e in range(3):
                first(d, c, e).wait_send()
                steps = half + 1 if far(c, e) == d else half
                lax.fori_loop(2, steps, lambda k, t: (forward(d, c, k, e).wait_send(), t)[1], 0)
                lax.fori_loop(1, steps, lambda m, t: (step_on(d, c, m, e).wait_send(), t)[1], 0)
    for copy in locals_ + swap + maps + stats + [give]:
        copy.wait_send()
    for c in (0, 1):
        for e in range(3):
            give_back(c, e).wait_send()
            give_back(c, e).wait_recv()
    out_copy.wait()


def per_device(nz, queries, store_kv, out_grad, neighbour_owner, neighbour_slot, neighbour_count):
    rows, width = queries.shape
    heads = width // HEAD_DIM
    ch = rows // SPAN
    half = nz // 2
    entries = store_kv.shape[1] // NLEN
    nt = lax.axis_size("tensor")
    bf, f32 = jnp.bfloat16, jnp.float32
    dma = pltpu.SemaphoreType.DMA
    block = (entries, NLEN, width)
    spans = (ch, SPAN, width)
    any_spec = pl.BlockSpec(memory_space=pl.ANY)
    attended, store_grad = pl.pallas_call(
        functools.partial(kernel, nz, nt, ch, heads),
        out_shape=[jax.ShapeDtypeStruct(spans, bf), jax.ShapeDtypeStruct((2,) + block, bf)],
        in_specs=[pl.BlockSpec(memory_space=pltpu.SMEM)] * 3 + [any_spec, any_spec, any_spec],
        out_specs=[any_spec, any_spec],
        scratch_shapes=[
            pltpu.VMEM((2, nz) + block, bf),
            pltpu.VMEM(spans, bf), pltpu.VMEM(spans, bf),
            pltpu.VMEM(spans, bf), pltpu.VMEM(spans, bf),
            pltpu.VMEM((nz * SLOTS, SPAN, width), f32),
            pltpu.VMEM((nz * SLOTS, SPAN, width), f32),
            pltpu.VMEM((2, 2, half + 1) + block, bf),
            pltpu.VMEM((2, 2) + block, f32),
            pltpu.VMEM((2,) + block, bf),
            pltpu.VMEM(spans, bf), pltpu.VMEM(spans, bf), pltpu.VMEM(spans, bf),
            pltpu.VMEM((2, SPAN, 128), f32), pltpu.VMEM((2, SPAN, 128), f32),
            pltpu.VMEM((2, SPAN, 128), f32), pltpu.VMEM((2, SPAN, 128), f32),
            pltpu.VMEM((2, SPAN, 128), f32), pltpu.VMEM((SPAN, 128), f32),
            dma((2, 2, half + 1, 3)), dma((2, 2, half + 1, 3)), dma((2,)), dma((2,)),
            dma((2,)), dma((2,)), dma((2,)), dma((2,)), dma((2,)),
            dma((2, 2, half + 1, 3)), dma((2, 2, half + 1, 3)), dma((1,)), dma((1,)),
            dma((2, 3)), dma((2, 3)), dma((1,)),
            pltpu.VMEM((2, nt, 8, 128), jnp.int32), pltpu.VMEM((nz, 128), jnp.int32),
            pltpu.VMEM((8, 128), jnp.int32), pltpu.SMEM((nz, 128), jnp.int32),
            pltpu.SMEM((8, 128), jnp.int32), dma((2, nt)), dma((2, nt)), dma((2,)),
        ],
        compiler_params=pltpu.CompilerParams(
            collective_id=0, has_side_effects=True, vmem_limit_bytes=60 * 1024 * 1024),
        cost_estimate=pl.CostEstimate(flops=4 * 10 ** 9, bytes_accessed=6 * 10 ** 6,
                                      transcendentals=4 * 10 ** 6),
    )(neighbour_owner, neighbour_slot, neighbour_count, queries.reshape(spans), store_kv.reshape((2,) + block), out_grad.reshape(spans))
    return attended.reshape(rows, width), store_grad.reshape(store_kv.shape)


def solution(mesh):
    nz = mesh.shape["seq"] // 2
    in_specs = (
        P(("section", "seq"), "tensor"),
        P(None, ("section", "seq"), "tensor"),
        P(("section", "seq"), "tensor"),
        P(("section", "seq", "tensor"), None),
        P(("section", "seq", "tensor"), None),
        P(("section", "seq", "tensor")),
    )
    out_specs = (P(("section", "seq"), "tensor"), P(None, ("section", "seq"), "tensor"))
    return jax.shard_map(
        functools.partial(per_device, nz), mesh=mesh, in_specs=in_specs, out_specs=out_specs,
        check_vma=False)
```

```python
import functools

import jax
import jax.numpy as jnp
from jax import lax
from jax.experimental import pallas as pl
from jax.experimental.pallas import tpu as pltpu
from jax.sharding import PartitionSpec as P

HEAD_DIM = 128
SPAN = 64
NLEN = 128
NEIGH = 2
SLOTS = 4
MESH = pl.DeviceIdType.MESH
DEAD = -1e30
NONE = -100000


def kernel(nz, nt, ch, heads, owner_in, entry_in, count_in, q_in, kv_in, g_in, att_out, sg_out,
           kv, q_own, q_nbr, g_own, g_nbr, pb, dpb, rs, cbuf, fin, asend, arecv, att,
           lse, gp, st_s, st_r, wts, dlt,
           ag_s, ag_r, loc_s, loc_r, qg_s, qg_r, own_l, stx_s, stx_r,
           rs_s, rs_r, a_s, a_r, f_s, f_r, o_l,
           meta, made, made_u, tab, tab_u, me_s, me_r, t_l,
           far_q, far_g, far_made, far_tab, far_st, far_a, fx_s, fx_r, ft_l):
    half = nz // 2
    stride = 2 * ch
    per_t = ch // nt
    scaling = HEAD_DIM ** (-0.5)
    q_blk, g_blk = (q_own, q_nbr), (g_own, g_nbr)
    sec = lax.axis_index("section")
    seq = lax.axis_index("seq")
    ten = lax.axis_index("tensor")
    y, z = lax.div(seq, nz), lax.rem(seq, nz)
    up, down = lax.rem(z + 1, nz), lax.rem(z + nz - 1, nz)
    z_to = (up, down)

    def dev(s, yy, zz):
        return {"section": s, "seq": yy * nz + zz}

    sibling = dev(1 - sec, y, z)
    y_nbr = dev(sec, 1 - y, z)

    def peer(b, dt):
        return {"seq": (y if b == 0 else 1 - y) * nz + z, "tensor": lax.rem(ten + dt, nt)}

    def remote(src, dst, ssem, rsem, device):
        return pltpu.make_async_remote_copy(
            src_ref=src, dst_ref=dst, send_sem=ssem, recv_sem=rsem,
            device_id=device, device_id_type=MESH)

    barrier = pltpu.get_barrier_semaphore()
    for device in (sibling, y_nbr, dev(sec, y, up), dev(sec, y, down),
                   dev(1 - sec, y, up), dev(1 - sec, y, down)) + tuple(
                       peer(b, dt) for b in (0, 1) for dt in range(1, nt)):
        pl.semaphore_signal(barrier, inc=1, device_id=device, device_id_type=MESH)
    own_q = pltpu.make_async_copy(q_in, q_own, own_l.at[0])
    own_g = pltpu.make_async_copy(g_in, g_own, own_l.at[1])
    own_q.start()
    own_g.start()
    lanes8 = lax.broadcasted_iota(jnp.int32, (8, 128), 1)
    rows8 = lax.broadcasted_iota(jnp.int32, (8, 128), 0)
    mine = jnp.zeros((8, 128), jnp.int32)
    for s in range(per_t):
        for j in range(NEIGH):
            at = lanes8 == (ten * per_t + s) * NEIGH + j
            for row, value in enumerate((owner_in[s, j], entry_in[s, j], count_in[s])):
                mine = jnp.where(jnp.logical_and(at, rows8 == row), value, mine)
    meta[0, ten] = mine
    pl.semaphore_wait(barrier, 6 + 2 * (nt - 1))

    def place(d, k):
        return nz - k if d == 0 else k

    def first(d, c, e):
        return remote(kv_in.at[c, e], kv.at[c, place(d, 1), e], ag_s.at[d, c, 1, e],
                      ag_r.at[d, c, 1, e], dev(1 - sec, y, z_to[d]))

    def forward(d, c, k, e):
        return remote(kv.at[c, place(d, k - 1), e], kv.at[c, place(d, k), e], ag_s.at[d, c, k, e],
                      ag_r.at[d, c, k, e], dev(sec, y, z_to[d]))

    def arrived(d, c, k, e):
        here = kv.at[c, place(d, k), e]
        remote(here, here, ag_s.at[d, c, k, e], ag_r.at[d, c, k, e],
               dev(sec, y, z_to[d])).wait_recv()

    def pass_on(c, k, e):
        for d in (0, 1):
            arrived(d, c, k, e)
            if not isinstance(k, int) or k < half - 1:
                forward(d, c, k + 1, e).start()

    def start_gather():
        for e in range(3):
            for c in (0, 1):
                for d in (0, 1):
                    first(d, c, e).start()

    start_gather()
    locals_ = [remote(kv_in.at[c], kv.at[c, 0], loc_s.at[c], loc_r.at[c], sibling) for c in (0, 1)]
    for copy in locals_:
        copy.start()
    maps = [remote(meta.at[0, ten], meta.at[b, ten], me_s.at[b, dt], me_r.at[b, dt],
                   peer(b, dt)) for dt in range(nt) for b in (0, 1) if b + dt > 0]
    for copy in maps:
        copy.start()
    swap = [remote(q_in, q_nbr, qg_s.at[0], qg_r.at[0], y_nbr),
            remote(g_in, g_nbr, qg_s.at[1], qg_r.at[1], y_nbr)]
    for copy in swap:
        copy.start()

    lse[...] = jnp.full_like(lse, DEAD)
    gp[...] = jnp.zeros_like(gp)
    lanes = lax.broadcasted_iota(jnp.int32, (SPAN, 128), 1)

    def build_tables():
        for dt in range(nt):
            for b in (0, 1):
                if b + dt > 0:
                    here = meta.at[b, lax.rem(ten + nt - dt, nt)]
                    remote(here, here, me_s.at[b, dt], me_r.at[b, dt], peer(b, dt)).wait_recv()
        unit = lax.broadcasted_iota(jnp.int32, (nz, 128), 1)
        row = lax.broadcasted_iota(jnp.int32, (nz, 128), 0)
        made_all = jnp.zeros((nz, 128), jnp.int32)
        unit_all = jnp.zeros((8, 128), jnp.int32)
        for b in (0, 1):
            whole = meta[b, 0]
            for t in range(1, nt):
                whole = whole + meta[b, t]
            spread = lambda i: jnp.broadcast_to(whole[i:i + 1], (nz, 128))
            owner, entry, count = spread(0), spread(1), spread(2)
            j_of = lax.bitwise_and(unit, 1)
            span = lax.shift_right_logical(unit, 1)
            col = owner - y * nz
            used = ((unit < ch * NEIGH) & (j_of < count)) & ((col >= 0) & (col < nz))
            rel = jnp.where(col < z, col - z + nz, col - z)
            mine = jnp.logical_and(used, rel == row)
            u0 = jnp.min(jnp.where(mine, unit, 1000), axis=1, keepdims=True)
            u1 = jnp.max(jnp.where(mine, unit, -1), axis=1, keepdims=True)
            u1 = jnp.where(u1 == u0, -1, u1)
            lane = (y if b == 0 else 1 - y) * ch + span
            for r, u in ((0, u0), (1, u1)):
                at = unit == u
                get = lambda v: jnp.sum(jnp.where(at, v, 0), axis=1, keepdims=True)
                values = (get(span), get(entry)) + tuple(
                    get(jnp.where(j_of == j, lane - NONE, 0)) + NONE for j in range(NEIGH))
                for i, value in enumerate(values):
                    made_all = jnp.where(unit == i * SLOTS + b * 2 + r, value, made_all)
            rank = jnp.sum(jnp.where(jnp.logical_and(mine, unit != u0), 1, 0), axis=0, keepdims=True)
            use1, rel1, entry1 = used[0:1], rel[0:1], entry[0:1]
            for i, value in enumerate((rel1, b * 2 + rank, entry1)):
                value = jnp.broadcast_to(jnp.where(use1, value, 0), (8, 128))
                unit_all = jnp.where(rows8 == b * 3 + i, value, unit_all)
        made[...] = made_all
        made_u[...] = unit_all
        copies = [pltpu.make_async_copy(made, tab, t_l.at[0]),
                  pltpu.make_async_copy(made_u, tab_u, t_l.at[1])]
        for copy in copies:
            copy.start()
        for copy in copies:
            copy.wait()

    def pick(three, es):
        return jnp.where(es == 0, three[0], jnp.where(es == 1, three[1], three[2]))

    def far_at(f):
        return half - 1 + 2 * f

    def far_copy(i, b, src, dst, back):
        return remote(src, dst, fx_s.at[i, b], fx_r.at[i, b],
                      dev(sec, y, z_to[1 - b] if back else z_to[b]))

    def far_spans(i, b):
        ref = (far_q, far_g)[i]
        return far_copy(i, b, ref.at[0, b], ref.at[1, b], False)

    def far_table(b):
        return far_copy(2, b, made, far_made.at[b], False)

    def far_tile(i, b):
        return far_copy(3 + i, b, far_st.at[0, i, b], far_st.at[1, i, b], i < 2)

    def far_part(b):
        return far_copy(7, b, far_a.at[0, b], far_a.at[1, b], True)

    def send_far():
        for b in (0, 1):
            for r in (0, 1):
                sp = tab[half, b * 2 + r]
                far_q[0, b, r] = q_blk[b][sp]
                far_g[0, b, r] = g_blk[b][sp]
        for b in (0, 1):
            far_table(b).start()
            far_spans(0, b).start()
            far_spans(1, b).start()

    def take_far():
        for b in (0, 1):
            far_table(b).wait_recv()
            pltpu.make_async_copy(far_made.at[b], far_tab.at[b], ft_l.at[b]).start()
        for b in (0, 1):
            pltpu.make_async_copy(far_made.at[b], far_tab.at[b], ft_l.at[b]).wait()
            far_spans(0, b).wait_recv()
            far_spans(1, b).wait_recv()

    def far_send(i, work):
        for f in (0, 1):
            tile = jnp.zeros((SPAN, 128), jnp.float32)
            for r in (0, 1):
                for h, value in enumerate(work(f, r)):
                    tile = jnp.where(lanes == r * heads + h, value, tile)
            far_st[0, i, f] = tile
            far_tile(i, f).start()

    def column(values, lane):
        return jnp.sum(jnp.where(lanes == lane, values, 0.0), axis=1, keepdims=True)

    def far_get(i, f, r, h):
        return column(far_st[1, i, f], r * heads + h)

    def far_insert(i, ref):
        for b in (0, 1):
            far_tile(i, b).wait_recv()
            for r in (0, 1):
                insert(ref, half, b * 2 + r, [far_get(i, b, r, h) for h in range(heads)])

    def place_of(n):
        return jnp.where(lax.rem(n, 2) == 1, nz - lax.div(n + 1, 2), lax.div(n, 2))

    def insert(ref, idx, slot, columns):
        for j in range(NEIGH):
            lane = tab[idx, (2 + j) * SLOTS + slot]
            a = ref[j]
            for h in range(heads):
                a = jnp.where(lanes == lane + h * stride, columns[h], a)
            ref[j] = a

    def score_slot(idx, sl, es, q_of):
        columns = []
        for h in range(heads):
            hs = pl.ds(h * HEAD_DIM, HEAD_DIM)
            ks = pick([kv[0, idx, e, :, hs] for e in range(3)], es)
            s = lax.dot_general(q_of(hs), ks, (((1,), (1,)), ((), ())),
                                preferred_element_type=jnp.float32) * scaling
            top = jnp.max(s, axis=1, keepdims=True)
            p = jnp.exp(s - top)
            tot = jnp.sum(p, axis=1, keepdims=True)
            pb[sl, :, hs] = p * (1.0 / tot)
            columns.append(top + jnp.log(tot))
        return columns

    def grad_slot(idx, sl, es, g_of):
        columns = []
        for h in range(heads):
            hs = pl.ds(h * HEAD_DIM, HEAD_DIM)
            vs = pick([kv[1, idx, e, :, hs] for e in range(3)], es)
            dp = lax.dot_general(g_of(hs), vs, (((1,), (1,)), ((), ())),
                                 preferred_element_type=jnp.float32)
            dpb[sl, :, hs] = dp
            columns.append(jnp.sum(pb[sl, :, hs] * dp, axis=1, keepdims=True))
        return columns

    def item(n, b, slot_work, rows, ref):
        idx = place_of(n)
        for r in (0, 1):
            slot = b * 2 + r
            sp = tab[idx, slot]
            insert(ref, idx, slot, slot_work(idx, idx * SLOTS + slot, tab[idx, SLOTS + slot],
                                             lambda hs: rows[b][sp, :, hs]))

    def far_entry(f, r):
        return far_tab[f, half, SLOTS + f * 2 + r]

    def far_slot(slot_work, rows):
        return lambda f, r: slot_work(far_at(f), half * SLOTS + f * 2 + r, far_entry(f, r),
                                      lambda hs: rows[1, f, r, :, hs])

    def score_item(n, b):
        item(n, b, score_slot, q_blk, lse)

    def grad_item(n, b):
        item(n, b, grad_slot, g_blk, gp)

    def items(work, lo, hi, b):
        lax.fori_loop(lo, hi, lambda n, t: (work(n, b), t)[1], 0)

    own_q.wait()
    own_g.wait()
    for copy in locals_:
        copy.wait_recv()
    build_tables()
    lag = 4

    def done(k):
        return jnp.maximum((k + 1 - lag) * 4, 0)

    def upto(step):
        return max(2 * step + 1, 0)

    def gather_step(k, t):
        pass_on(0, k, 0)
        items(score_item, jnp.maximum(2 * k - 3, 0), 2 * k - 1, 0)
        pass_on(1, k, 0)

        @pl.when(k == lag)
        def _():
            for copy in swap:
                copy.wait_recv()
            send_far()

        lo, hi = done(k - 1), done(k)
        mid = jnp.minimum(lo + 2, hi)
        items(score_item, lo, mid, 1)
        pass_on(0, k, 1)
        items(score_item, mid, hi, 1)
        pass_on(1, k, 1)
        items(grad_item, lo, hi, 0)
        pass_on(0, k, 2)
        items(grad_item, lo, hi, 1)
        pass_on(1, k, 2)
        return t

    both = half - 4
    lax.fori_loop(1, both + 1, gather_step, 0)
    if both < lag:
        for copy in swap:
            copy.wait_recv()
        send_far()
    own_at = upto(both - 1)
    nbr_at = max((both + 1 - lag) * 4, 0)
    for k in range(max(half - 3, 1), half - 1):
        for e in range(3):
            pass_on(0, k, e)
    if half > 3:
        pass_on(1, half - 3, 0)
    for b in (0, 1):
        items(score_item, own_at if b == 0 else nbr_at, upto(half - 2), b)
    take_far()
    for e in range(3):
        pass_on(0, half - 1, e)
    far_send(0, far_slot(score_slot, far_q))
    if half > 3:
        pass_on(1, half - 3, 1)
        pass_on(1, half - 3, 2)
    for b in (0, 1):
        items(score_item, upto(half - 2), upto(half - 1), b)
    far_insert(0, lse)

    def exchange(i, value):
        st_s[i] = value
        copy = remote(st_s.at[i], st_r.at[i], stx_s.at[i], stx_r.at[i], y_nbr)
        copy.start()
        copy.wait_recv()
        return copy

    a0, a1 = lse[0], lse[1]
    top = jnp.maximum(a0, a1)
    lc = top + jnp.log(jnp.exp(a0 - top) + jnp.exp(a1 - top))
    stats = [exchange(0, lc)]
    lo_ = st_r[0]
    top = jnp.maximum(lc, lo_)
    total = top + jnp.log(jnp.exp(lc - top) + jnp.exp(lo_ - top))
    wts[0] = jnp.exp(a0 - total)
    wts[1] = jnp.exp(a1 - total)

    def slot_lanes(idx, slot, h):
        return (tab[idx, 2 * SLOTS + slot] + h * stride, tab[idx, 3 * SLOTS + slot] + h * stride)

    def weight(lane0, lane1):
        w = jnp.where(lanes == lane0, wts[0], 0.0) + jnp.where(lanes == lane1, wts[1], 0.0)
        return jnp.sum(w, axis=1, keepdims=True)

    far_send(2, lambda b, r: [weight(*slot_lanes(half, b * 2 + r, h)) for h in range(heads)])
    if half > 2:
        pass_on(1, half - 2, 0)
        pass_on(1, half - 2, 1)

    def contribution(c, idx, h, f=None):
        hs = pl.ds(h * HEAD_DIM, HEAD_DIM)
        left, right = [], []
        for slot in range(SLOTS) if f is None else range(SLOTS, SLOTS + 2):
            if slot < SLOTS:
                sl = idx * SLOTS + slot
                sp, es = tab[idx, slot], tab[idx, SLOTS + slot]
                l0, l1 = slot_lanes(idx, slot, h)
                w = weight(l0, l1)
                rows = (q_blk, g_blk)[c][slot // 2][sp, :, hs]
            else:
                r = slot - SLOTS
                sl = half * SLOTS + f * 2 + r
                es = far_entry(f, r)
                w = far_get(2, f, r, h)
                rows = (far_q, far_g)[c][1, f, r, :, hs]
            p = pb[sl, :, hs] * w
            if c == 0:
                delta = (column(dlt[...], jnp.maximum(l0, l1)) if slot < SLOTS
                         else far_get(3, f, r, h))
                p = p * (dpb[sl, :, hs] - delta)
            right.append(rows)
            x = p.astype(jnp.bfloat16)
            zero = jnp.zeros_like(x)
            left.append(jnp.concatenate([jnp.where(es == e, x, zero) for e in range(3)], axis=1))
        out = lax.dot_general(jnp.concatenate(left, axis=0), jnp.concatenate(right, axis=0),
                              (((0,), (0,)), ((), ())), preferred_element_type=jnp.float32)
        if c == 0:
            out = out * scaling
        return out.reshape(3, NLEN, HEAD_DIM)

    def contribute(c, idx, into):
        for h in range(heads):
            cbuf[c, into, :, :, pl.ds(h * HEAD_DIM, HEAD_DIM)] = contribution(c, idx, h)

    def step_on(d, c, m, e):
        return remote(rs.at[d, c, m, e], rs.at[d, c, m - 1, e], rs_s.at[d, c, m - 1, e],
                      rs_r.at[d, c, m - 1, e], dev(sec, y, z_to[d]))

    def sum_arrived(d, c, m, e):
        here = rs.at[d, c, m, e]
        remote(here, here, rs_s.at[d, c, m, e], rs_r.at[d, c, m, e], y_nbr).wait_recv()

    def contribute_both(c, m):
        lax.fori_loop(0, 2, lambda d, t: (contribute(c, jnp.where(d == 0, m, nz - m), d), t)[1], 0)

    def far_contribute(c):
        for d in (0, 1):
            for h in range(heads):
                hs = pl.ds(h * HEAD_DIM, HEAD_DIM)
                o = cbuf[c, d, :, :, hs] + contribution(c, far_at(d), h, d)
                rs[d, c, half - 1, :, :, hs] = o.astype(jnp.bfloat16)

    def start_sums(c, entries):
        for e in entries:
            for d in (0, 1):
                step_on(d, c, half - 1, e).start()

    def add_on(c, d, m, e):
        sum_arrived(d, c, m, e)
        o = cbuf[c, d, e] + rs[d, c, m, e].astype(jnp.float32)
        rs[d, c, m, e] = o.astype(jnp.bfloat16)
        step_on(d, c, m, e).start()

    def last_sum(c, e):
        sum_arrived(0, c, 0, e)
        sum_arrived(1, c, 0, e)
        o = cbuf[c, 0, e] + (rs[0, c, 0, e].astype(jnp.float32) + rs[1, c, 0, e].astype(jnp.float32))
        fin[c, e] = o.astype(jnp.bfloat16)
        give_back(c, e).start()

    def give_back(c, e):
        return remote(fin.at[c, e], sg_out.at[c, e], f_s.at[c, e], f_r.at[c, e], sibling)

    def attended_span(b, sp):
        y_b = y if b == 0 else 1 - y
        outs = []
        for h in range(heads):
            hs = pl.ds(h * HEAD_DIM, HEAD_DIM)
            acc = jnp.zeros((SPAN, HEAD_DIM), jnp.float32)
            for j in range(NEIGH):
                at = sp * NEIGH + j
                idx = tab_u[b * 3, at]
                sl = idx * SLOTS + tab_u[b * 3 + 1, at]
                es = tab_u[b * 3 + 2, at]
                w = column(wts[j], y_b * ch + sp + h * stride)
                p = (pb[sl, :, hs] * w).astype(jnp.bfloat16)
                near = jnp.dot(p, kv[1, idx, es, :, hs], preferred_element_type=jnp.float32)
                away = far_a[1, b, lax.rem(tab_u[b * 3 + 1, at], 2), :, hs].astype(jnp.float32)
                acc += jnp.where(idx == half, away, near)
            outs.append((hs, acc))
        return outs

    def nbr_span(sp, t):
        for hs, acc in attended_span(1, sp):
            asend[sp, :, hs] = acc.astype(jnp.bfloat16)
        return t

    def own_span(sp, t):
        for hs, acc in attended_span(0, sp):
            both = acc + arecv[sp, :, hs].astype(jnp.float32)
            att[sp, :, hs] = both.astype(jnp.bfloat16)
        return t

    give = remote(asend, arecv, a_s.at[0], a_r.at[0], y_nbr)
    out_copy = pltpu.make_async_copy(att, att_out, o_l.at[0])

    contribute_both(1, half - 1)
    if half > 2:
        pass_on(1, half - 2, 2)
    for f in (0, 1):
        far_tile(2, f).wait_recv()
    far_contribute(1)
    for b in (0, 1):
        items(grad_item, nbr_at, upto(half - 2), b)
    start_sums(1, (0,))
    for e in range(3):
        pass_on(1, half - 1, e)
    far_send(1, far_slot(grad_slot, far_g))
    start_sums(1, (1,))
    for b in (0, 1):
        items(grad_item, upto(half - 2), upto(half - 1), b)
    far_insert(1, gp)
    gc = wts[0] * gp[0] + wts[1] * gp[1]
    stats.append(exchange(1, gc))
    dlt[...] = gc + st_r[1]
    far_send(3, lambda b, r: [
        column(dlt[...], jnp.maximum(*slot_lanes(half, b * 2 + r, h))) for h in range(heads)])
    start_sums(1, (2,))
    contribute_both(0, half - 1)

    for f in (0, 1):
        for r in (0, 1):
            for h in range(heads):
                hs = pl.ds(h * HEAD_DIM, HEAD_DIM)
                p = (pb[half * SLOTS + f * 2 + r, :, hs] * far_get(2, f, r, h)).astype(jnp.bfloat16)
                o = jnp.dot(p, kv[1, far_at(f), far_entry(f, r), :, hs],
                            preferred_element_type=jnp.float32)
                far_a[0, f, r, :, hs] = o.astype(jnp.bfloat16)
    for f in (0, 1):
        far_tile(3, f).wait_recv()
    far_contribute(0)
    start_sums(0, (0, 1, 2))
    for f in (0, 1):
        far_part(f).start()

    def spans(k):
        if half < 8:
            return

        @pl.when(k == 2)
        def _():
            for f in (0, 1):
                far_part(f).wait_recv()

        @pl.when(k <= 3)
        def _():
            lax.fori_loop((k - 2) * (ch // 2), (k - 1) * (ch // 2), nbr_span, 0)

        @pl.when(k == 3)
        def _():
            give.start()

        @pl.when(k == 6)
        def _():
            give.wait_recv()

        @pl.when(jnp.logical_and(k >= 6, k <= 7))
        def _():
            lax.fori_loop((k - 6) * (ch // 2), (k - 5) * (ch // 2), own_span, 0)

        @pl.when(k == 7)
        def _():
            out_copy.start()

    def early_sent(c):
        for d in (0, 1):
            for e in range(3):
                first(d, c, e).wait_send()
                lax.fori_loop(2, half, lambda k, t: (forward(d, c, k, e).wait_send(), t)[1], 0)

    def small_sent():
        for b in (0, 1):
            for copy in ([far_spans(0, b), far_spans(1, b), far_table(b), far_part(b)]
                         + [far_tile(i, b) for i in range(4)]):
                copy.wait_send()
        for copy in locals_ + swap + maps + stats + [give]:
            copy.wait_send()

    def sums_sent(m):
        for c in (0, 1):
            for d in (0, 1):
                for e in range(3):
                    step_on(d, c, m, e).wait_send()

    def sum_step(k, t):
        m = half - k
        contribute_both(1, m)
        contribute_both(0, m)
        for e in range(3):
            for c in (1, 0):
                for d in (0, 1):
                    add_on(c, d, m, e)
        spans(k)
        if half >= 8:
            pl.when(k == 4)(lambda: early_sent(0))
            pl.when(k == 5)(lambda: early_sent(1))
            pl.when(k == 7)(small_sent)

        @pl.when(k >= 3)
        def _():
            sums_sent(m + 2)

        return t

    lax.fori_loop(2, half, sum_step, 0)
    if half < 8:
        for f in (0, 1):
            far_part(f).wait_recv()
        lax.fori_loop(0, ch, nbr_span, 0)
        give.start()
        give.wait_recv()
        lax.fori_loop(0, ch, own_span, 0)
        out_copy.start()
    contribute(1, 0, 0)
    contribute(0, 0, 0)
    for e in range(3):
        for c in (1, 0):
            last_sum(c, e)

    if half < 8:
        early_sent(0)
        early_sent(1)
        small_sent()
    for m in sorted({1, min(2, half - 1)}):
        sums_sent(m)
    for c in (0, 1):
        for e in range(3):
            give_back(c, e).wait_send()
            give_back(c, e).wait_recv()
    out_copy.wait()


def per_device(nz, queries, store_kv, out_grad, neighbour_owner, neighbour_slot, neighbour_count):
    rows, width = queries.shape
    heads = width // HEAD_DIM
    ch = rows // SPAN
    half = nz // 2
    entries = store_kv.shape[1] // NLEN
    nt = lax.axis_size("tensor")
    bf, f32 = jnp.bfloat16, jnp.float32
    dma = pltpu.SemaphoreType.DMA
    block = (entries, NLEN, width)
    spans = (ch, SPAN, width)
    any_spec = pl.BlockSpec(memory_space=pl.ANY)
    attended, store_grad = pl.pallas_call(
        functools.partial(kernel, nz, nt, ch, heads),
        out_shape=[jax.ShapeDtypeStruct(spans, bf), jax.ShapeDtypeStruct((2,) + block, bf)],
        in_specs=[pl.BlockSpec(memory_space=pltpu.SMEM)] * 3 + [any_spec, any_spec, any_spec],
        out_specs=[any_spec, any_spec],
        scratch_shapes=[
            pltpu.VMEM((2, nz) + block, bf),
            pltpu.VMEM(spans, bf), pltpu.VMEM(spans, bf),
            pltpu.VMEM(spans, bf), pltpu.VMEM(spans, bf),
            pltpu.VMEM((nz * SLOTS, SPAN, width), f32),
            pltpu.VMEM((nz * SLOTS, SPAN, width), f32),
            pltpu.VMEM((2, 2, half + 1) + block, bf),
            pltpu.VMEM((2, 2) + block, f32),
            pltpu.VMEM((2,) + block, bf),
            pltpu.VMEM(spans, bf), pltpu.VMEM(spans, bf), pltpu.VMEM(spans, bf),
            pltpu.VMEM((2, SPAN, 128), f32), pltpu.VMEM((2, SPAN, 128), f32),
            pltpu.VMEM((2, SPAN, 128), f32), pltpu.VMEM((2, SPAN, 128), f32),
            pltpu.VMEM((2, SPAN, 128), f32), pltpu.VMEM((SPAN, 128), f32),
            dma((2, 2, half + 1, 3)), dma((2, 2, half + 1, 3)), dma((2,)), dma((2,)),
            dma((2,)), dma((2,)), dma((2,)), dma((2,)), dma((2,)),
            dma((2, 2, half + 1, 3)), dma((2, 2, half + 1, 3)), dma((1,)), dma((1,)),
            dma((2, 3)), dma((2, 3)), dma((1,)),
            pltpu.VMEM((2, nt, 8, 128), jnp.int32), pltpu.VMEM((nz, 128), jnp.int32),
            pltpu.VMEM((8, 128), jnp.int32), pltpu.SMEM((nz, 128), jnp.int32),
            pltpu.SMEM((8, 128), jnp.int32), dma((2, nt)), dma((2, nt)), dma((2,)),
            pltpu.VMEM((2, 2, 2, SPAN, width), bf), pltpu.VMEM((2, 2, 2, SPAN, width), bf),
            pltpu.VMEM((2, nz, 128), jnp.int32), pltpu.SMEM((2, nz, 128), jnp.int32),
            pltpu.VMEM((2, 4, 2, SPAN, 128), f32), pltpu.VMEM((2, 2, 2, SPAN, width), bf),
            dma((8, 2)), dma((8, 2)), dma((2,)),
        ],
        compiler_params=pltpu.CompilerParams(
            collective_id=0, has_side_effects=True, vmem_limit_bytes=60 * 1024 * 1024),
        cost_estimate=pl.CostEstimate(flops=4 * 10 ** 9, bytes_accessed=6 * 10 ** 6,
                                      transcendentals=4 * 10 ** 6),
    )(neighbour_owner, neighbour_slot, neighbour_count, queries.reshape(spans), store_kv.reshape((2,) + block), out_grad.reshape(spans))
    return attended.reshape(rows, width), store_grad.reshape(store_kv.shape)


def solution(mesh):
    nz = mesh.shape["seq"] // 2
    in_specs = (
        P(("section", "seq"), "tensor"),
        P(None, ("section", "seq"), "tensor"),
        P(("section", "seq"), "tensor"),
        P(("section", "seq", "tensor"), None),
        P(("section", "seq", "tensor"), None),
        P(("section", "seq", "tensor")),
    )
    out_specs = (P(("section", "seq"), "tensor"), P(None, ("section", "seq"), "tensor"))
    return jax.shard_map(
        functools.partial(per_device, nz), mesh=mesh, in_specs=in_specs, out_specs=out_specs,
        check_vma=False)
```

```python
import functools

import jax
import jax.numpy as jnp
from jax import lax
from jax.experimental import pallas as pl
from jax.experimental.pallas import tpu as pltpu
from jax.sharding import PartitionSpec as P

HEAD_DIM = 128
SPAN = 64
NLEN = 128
NEIGH = 2
SLOTS = 4
MESH = pl.DeviceIdType.MESH
DEAD = -1e30
NONE = -100000
PIECES = 4


def kernel(nz, nt, ch, heads, owner_in, entry_in, count_in, q_in, kv_in, g_in, att_out, sg_out,
           kv, q_own, q_nbr, g_own, g_nbr, pb, dpb, rs, cbuf, fin, asend, arecv, att,
           lse, gp, st_s, st_r, wts, dlt,
           ag_s, ag_r, loc_s, loc_r, qg_s, qg_r, own_l, stx_s, stx_r,
           rs_s, rs_r, a_s, a_r, f_s, f_r, o_l,
           meta, made, made_u, tab, tab_u, me_s, me_r, t_l,
           far_q, far_g, far_made, far_tab, far_st, far_a, fx_s, fx_r, ft_l):
    half = nz // 2
    stride = 2 * ch
    per_t = ch // nt
    scaling = HEAD_DIM ** (-0.5)
    q_blk, g_blk = (q_own, q_nbr), (g_own, g_nbr)
    sec = lax.axis_index("section")
    seq = lax.axis_index("seq")
    ten = lax.axis_index("tensor")
    y, z = lax.div(seq, nz), lax.rem(seq, nz)
    up, down = lax.rem(z + 1, nz), lax.rem(z + nz - 1, nz)
    z_to = (up, down)

    def dev(s, yy, zz):
        return {"section": s, "seq": yy * nz + zz}

    sibling = dev(1 - sec, y, z)
    y_nbr = dev(sec, 1 - y, z)

    def peer(b, dt):
        return {"seq": (y if b == 0 else 1 - y) * nz + z, "tensor": lax.rem(ten + dt, nt)}

    def remote(src, dst, ssem, rsem, device):
        return pltpu.make_async_remote_copy(
            src_ref=src, dst_ref=dst, send_sem=ssem, recv_sem=rsem,
            device_id=device, device_id_type=MESH)

    barrier = pltpu.get_barrier_semaphore()
    for device in (sibling, y_nbr, dev(sec, y, up), dev(sec, y, down),
                   dev(1 - sec, y, up), dev(1 - sec, y, down)) + tuple(
                       peer(b, dt) for b in (0, 1) for dt in range(1, nt)):
        pl.semaphore_signal(barrier, inc=1, device_id=device, device_id_type=MESH)
    own_q = pltpu.make_async_copy(q_in, q_own, own_l.at[0])
    own_g = pltpu.make_async_copy(g_in, g_own, own_l.at[1])
    own_q.start()
    own_g.start()
    lanes8 = lax.broadcasted_iota(jnp.int32, (8, 128), 1)
    rows8 = lax.broadcasted_iota(jnp.int32, (8, 128), 0)
    mine = jnp.zeros((8, 128), jnp.int32)
    for s in range(per_t):
        for j in range(NEIGH):
            at = lanes8 == (ten * per_t + s) * NEIGH + j
            for row, value in enumerate((owner_in[s, j], entry_in[s, j], count_in[s])):
                mine = jnp.where(jnp.logical_and(at, rows8 == row), value, mine)
    meta[0, ten] = mine
    pl.semaphore_wait(barrier, 6 + 2 * (nt - 1))

    def place(d, k):
        return nz - k if d == 0 else k

    def first(d, c, e):
        return remote(kv_in.at[c, e], kv.at[c, place(d, 1), e], ag_s.at[d, c, 1, e],
                      ag_r.at[d, c, 1, e], dev(1 - sec, y, z_to[d]))

    def forward(d, c, k, e):
        return remote(kv.at[c, place(d, k - 1), e], kv.at[c, place(d, k), e], ag_s.at[d, c, k, e],
                      ag_r.at[d, c, k, e], dev(sec, y, z_to[d]))

    def arrived(d, c, k, e):
        here = kv.at[c, place(d, k), e]
        remote(here, here, ag_s.at[d, c, k, e], ag_r.at[d, c, k, e],
               dev(sec, y, z_to[d])).wait_recv()

    def pass_on(c, k, e):
        for d in (0, 1):
            arrived(d, c, k, e)
            if not isinstance(k, int) or k < half - 1:
                forward(d, c, k + 1, e).start()

    def start_gather():
        for e in range(3):
            for c in (0, 1):
                for d in (0, 1):
                    first(d, c, e).start()

    start_gather()
    locals_ = [remote(kv_in.at[c], kv.at[c, 0], loc_s.at[c], loc_r.at[c], sibling) for c in (0, 1)]
    for copy in locals_:
        copy.start()
    maps = [remote(meta.at[0, ten], meta.at[b, ten], me_s.at[b, dt], me_r.at[b, dt],
                   peer(b, dt)) for dt in range(nt) for b in (0, 1) if b + dt > 0]
    for copy in maps:
        copy.start()
    swap = [remote(q_in, q_nbr, qg_s.at[0], qg_r.at[0], y_nbr),
            remote(g_in, g_nbr, qg_s.at[1], qg_r.at[1], y_nbr)]
    for copy in swap:
        copy.start()

    lse[...] = jnp.full_like(lse, DEAD)
    gp[...] = jnp.zeros_like(gp)
    lanes = lax.broadcasted_iota(jnp.int32, (SPAN, 128), 1)

    def build_tables():
        for dt in range(nt):
            for b in (0, 1):
                if b + dt > 0:
                    here = meta.at[b, lax.rem(ten + nt - dt, nt)]
                    remote(here, here, me_s.at[b, dt], me_r.at[b, dt], peer(b, dt)).wait_recv()
        unit = lax.broadcasted_iota(jnp.int32, (nz, 128), 1)
        row = lax.broadcasted_iota(jnp.int32, (nz, 128), 0)
        made_all = jnp.zeros((nz, 128), jnp.int32)
        unit_all = jnp.zeros((8, 128), jnp.int32)
        for b in (0, 1):
            whole = meta[b, 0]
            for t in range(1, nt):
                whole = whole + meta[b, t]
            spread = lambda i: jnp.broadcast_to(whole[i:i + 1], (nz, 128))
            owner, entry, count = spread(0), spread(1), spread(2)
            j_of = lax.bitwise_and(unit, 1)
            span = lax.shift_right_logical(unit, 1)
            col = owner - y * nz
            used = ((unit < ch * NEIGH) & (j_of < count)) & ((col >= 0) & (col < nz))
            rel = jnp.where(col < z, col - z + nz, col - z)
            mine = jnp.logical_and(used, rel == row)
            u0 = jnp.min(jnp.where(mine, unit, 1000), axis=1, keepdims=True)
            u1 = jnp.max(jnp.where(mine, unit, -1), axis=1, keepdims=True)
            u1 = jnp.where(u1 == u0, -1, u1)
            lane = (y if b == 0 else 1 - y) * ch + span
            for r, u in ((0, u0), (1, u1)):
                at = unit == u
                get = lambda v: jnp.sum(jnp.where(at, v, 0), axis=1, keepdims=True)
                values = (get(span), get(entry)) + tuple(
                    get(jnp.where(j_of == j, lane - NONE, 0)) + NONE for j in range(NEIGH))
                for i, value in enumerate(values):
                    made_all = jnp.where(unit == i * SLOTS + b * 2 + r, value, made_all)
            rank = jnp.sum(jnp.where(jnp.logical_and(mine, unit != u0), 1, 0), axis=0, keepdims=True)
            use1, rel1, entry1 = used[0:1], rel[0:1], entry[0:1]
            for i, value in enumerate((rel1, b * 2 + rank, entry1)):
                value = jnp.broadcast_to(jnp.where(use1, value, 0), (8, 128))
                unit_all = jnp.where(rows8 == b * 3 + i, value, unit_all)
        made[...] = made_all
        made_u[...] = unit_all
        copies = [pltpu.make_async_copy(made, tab, t_l.at[0]),
                  pltpu.make_async_copy(made_u, tab_u, t_l.at[1])]
        for copy in copies:
            copy.start()
        for copy in copies:
            copy.wait()

    def pick(three, es):
        return jnp.where(es == 0, three[0], jnp.where(es == 1, three[1], three[2]))

    def far_at(f):
        return half - 1 + 2 * f

    def far_copy(i, b, src, dst, back):
        return remote(src, dst, fx_s.at[i, b], fx_r.at[i, b],
                      dev(sec, y, z_to[1 - b] if back else z_to[b]))

    def far_spans(i, b):
        ref = (far_q, far_g)[i]
        return far_copy(i, b, ref.at[0, b], ref.at[1, b], False)

    def far_table(b):
        return far_copy(2, b, made, far_made.at[b], False)

    def far_tile(i, b):
        return far_copy(3 + i, b, far_st.at[0, i, b], far_st.at[1, i, b], i < 2)

    def far_part(b):
        return far_copy(7, b, far_a.at[0, b], far_a.at[1, b], True)

    def send_far():
        for b in (0, 1):
            for r in (0, 1):
                sp = tab[half, b * 2 + r]
                far_q[0, b, r] = q_blk[b][sp]
                far_g[0, b, r] = g_blk[b][sp]
        for b in (0, 1):
            far_table(b).start()
            far_spans(0, b).start()
            far_spans(1, b).start()

    def take_far():
        for b in (0, 1):
            far_table(b).wait_recv()
            pltpu.make_async_copy(far_made.at[b], far_tab.at[b], ft_l.at[b]).start()
        for b in (0, 1):
            pltpu.make_async_copy(far_made.at[b], far_tab.at[b], ft_l.at[b]).wait()
            far_spans(0, b).wait_recv()
            far_spans(1, b).wait_recv()

    def far_send(i, work):
        for f in (0, 1):
            tile = jnp.zeros((SPAN, 128), jnp.float32)
            for r in (0, 1):
                for h, value in enumerate(work(f, r)):
                    tile = jnp.where(lanes == r * heads + h, value, tile)
            far_st[0, i, f] = tile
            far_tile(i, f).start()

    def column(values, lane):
        return jnp.sum(jnp.where(lanes == lane, values, 0.0), axis=1, keepdims=True)

    def far_get(i, f, r, h):
        return column(far_st[1, i, f], r * heads + h)

    def far_insert(i, ref):
        for b in (0, 1):
            far_tile(i, b).wait_recv()
            for r in (0, 1):
                insert(ref, half, b * 2 + r, [far_get(i, b, r, h) for h in range(heads)])

    def place_of(n):
        return jnp.where(lax.rem(n, 2) == 1, nz - lax.div(n + 1, 2), lax.div(n, 2))

    def insert(ref, idx, slot, columns):
        for j in range(NEIGH):
            lane = tab[idx, (2 + j) * SLOTS + slot]
            a = ref[j]
            for h in range(heads):
                a = jnp.where(lanes == lane + h * stride, columns[h], a)
            ref[j] = a

    def score_slot(idx, sl, es, q_of):
        columns = []
        for h in range(heads):
            hs = pl.ds(h * HEAD_DIM, HEAD_DIM)
            ks = pick([kv[0, idx, e, :, hs] for e in range(3)], es)
            s = lax.dot_general(q_of(hs), ks, (((1,), (1,)), ((), ())),
                                preferred_element_type=jnp.float32) * scaling
            top = jnp.max(s, axis=1, keepdims=True)
            p = jnp.exp(s - top)
            tot = jnp.sum(p, axis=1, keepdims=True)
            pb[sl, :, hs] = p * (1.0 / tot)
            columns.append(top + jnp.log(tot))
        return columns

    def grad_slot(idx, sl, es, g_of):
        columns = []
        for h in range(heads):
            hs = pl.ds(h * HEAD_DIM, HEAD_DIM)
            vs = pick([kv[1, idx, e, :, hs] for e in range(3)], es)
            dp = lax.dot_general(g_of(hs), vs, (((1,), (1,)), ((), ())),
                                 preferred_element_type=jnp.float32)
            dpb[sl, :, hs] = dp
            columns.append(jnp.sum(pb[sl, :, hs] * dp, axis=1, keepdims=True))
        return columns

    def item(n, b, slot_work, rows, ref):
        idx = place_of(n)
        for r in (0, 1):
            slot = b * 2 + r
            sp = tab[idx, slot]
            insert(ref, idx, slot, slot_work(idx, idx * SLOTS + slot, tab[idx, SLOTS + slot],
                                             lambda hs: rows[b][sp, :, hs]))

    def far_entry(f, r):
        return far_tab[f, half, SLOTS + f * 2 + r]

    def far_slot(slot_work, rows):
        return lambda f, r: slot_work(far_at(f), half * SLOTS + f * 2 + r, far_entry(f, r),
                                      lambda hs: rows[1, f, r, :, hs])

    def score_item(n, b):
        item(n, b, score_slot, q_blk, lse)

    def grad_item(n, b):
        item(n, b, grad_slot, g_blk, gp)

    def items(work, lo, hi, b):
        lax.fori_loop(lo, hi, lambda n, t: (work(n, b), t)[1], 0)

    own_q.wait()
    own_g.wait()
    for copy in locals_:
        copy.wait_recv()
    build_tables()
    lag = 4

    def done(k):
        return jnp.maximum((k + 1 - lag) * 4, 0)

    def upto(step):
        return max(2 * step + 1, 0)

    def gather_step(k, t):
        pass_on(0, k, 0)
        items(score_item, jnp.maximum(2 * k - 3, 0), 2 * k - 1, 0)
        pass_on(1, k, 0)

        @pl.when(k == lag)
        def _():
            for copy in swap:
                copy.wait_recv()
            send_far()

        lo, hi = done(k - 1), done(k)
        mid = jnp.minimum(lo + 2, hi)
        items(score_item, lo, mid, 1)
        pass_on(0, k, 1)
        items(score_item, mid, hi, 1)
        pass_on(1, k, 1)
        items(grad_item, lo, hi, 0)
        pass_on(0, k, 2)
        items(grad_item, lo, hi, 1)
        pass_on(1, k, 2)
        return t

    both = half - 4
    lax.fori_loop(1, both + 1, gather_step, 0)
    if both < lag:
        for copy in swap:
            copy.wait_recv()
        send_far()
    own_at = upto(both - 1)
    nbr_at = max((both + 1 - lag) * 4, 0)
    for k in range(max(half - 3, 1), half - 1):
        for e in range(3):
            pass_on(0, k, e)
    if half > 3:
        pass_on(1, half - 3, 0)
    for b in (0, 1):
        items(score_item, own_at if b == 0 else nbr_at, upto(half - 2), b)
    take_far()
    for e in range(3):
        pass_on(0, half - 1, e)
    far_send(0, far_slot(score_slot, far_q))
    if half > 3:
        pass_on(1, half - 3, 1)
        pass_on(1, half - 3, 2)
    for b in (0, 1):
        items(score_item, upto(half - 2), upto(half - 1), b)
    far_insert(0, lse)

    def exchange(i, value):
        st_s[i] = value
        copy = remote(st_s.at[i], st_r.at[i], stx_s.at[i], stx_r.at[i], y_nbr)
        copy.start()
        copy.wait_recv()
        return copy

    a0, a1 = lse[0], lse[1]
    top = jnp.maximum(a0, a1)
    lc = top + jnp.log(jnp.exp(a0 - top) + jnp.exp(a1 - top))
    stats = [exchange(0, lc)]
    lo_ = st_r[0]
    top = jnp.maximum(lc, lo_)
    total = top + jnp.log(jnp.exp(lc - top) + jnp.exp(lo_ - top))
    wts[0] = jnp.exp(a0 - total)
    wts[1] = jnp.exp(a1 - total)

    def slot_lanes(idx, slot, h):
        return (tab[idx, 2 * SLOTS + slot] + h * stride, tab[idx, 3 * SLOTS + slot] + h * stride)

    def weight(lane0, lane1):
        w = jnp.where(lanes == lane0, wts[0], 0.0) + jnp.where(lanes == lane1, wts[1], 0.0)
        return jnp.sum(w, axis=1, keepdims=True)

    far_send(2, lambda b, r: [weight(*slot_lanes(half, b * 2 + r, h)) for h in range(heads)])
    if half > 2:
        pass_on(1, half - 2, 0)
        pass_on(1, half - 2, 1)

    def contribution(c, idx, h, f=None):
        hs = pl.ds(h * HEAD_DIM, HEAD_DIM)
        left, right = [], []
        for slot in range(SLOTS) if f is None else range(SLOTS, SLOTS + 2):
            if slot < SLOTS:
                sl = idx * SLOTS + slot
                sp, es = tab[idx, slot], tab[idx, SLOTS + slot]
                l0, l1 = slot_lanes(idx, slot, h)
                w = weight(l0, l1)
                rows = (q_blk, g_blk)[c][slot // 2][sp, :, hs]
            else:
                r = slot - SLOTS
                sl = half * SLOTS + f * 2 + r
                es = far_entry(f, r)
                w = far_get(2, f, r, h)
                rows = (far_q, far_g)[c][1, f, r, :, hs]
            p = pb[sl, :, hs] * w
            if c == 0:
                delta = (column(dlt[...], jnp.maximum(l0, l1)) if slot < SLOTS
                         else far_get(3, f, r, h))
                p = p * (dpb[sl, :, hs] - delta)
            right.append(rows)
            x = p.astype(jnp.bfloat16)
            zero = jnp.zeros_like(x)
            left.append(jnp.concatenate([jnp.where(es == e, x, zero) for e in range(3)], axis=1))
        out = lax.dot_general(jnp.concatenate(left, axis=0), jnp.concatenate(right, axis=0),
                              (((0,), (0,)), ((), ())), preferred_element_type=jnp.float32)
        if c == 0:
            out = out * scaling
        return out.reshape(3, NLEN, HEAD_DIM)

    def contribute(c, idx, into):
        for h in range(heads):
            cbuf[c, into, :, :, pl.ds(h * HEAD_DIM, HEAD_DIM)] = contribution(c, idx, h)

    def step_on(d, c, m, e):
        return remote(rs.at[d, c, m, e], rs.at[d, c, m - 1, e], rs_s.at[d, c, m - 1, e],
                      rs_r.at[d, c, m - 1, e], dev(sec, y, z_to[d]))

    def sum_arrived(d, c, m, e):
        here = rs.at[d, c, m, e]
        remote(here, here, rs_s.at[d, c, m, e], rs_r.at[d, c, m, e], y_nbr).wait_recv()

    def contribute_both(c, m):
        lax.fori_loop(0, 2, lambda d, t: (contribute(c, jnp.where(d == 0, m, nz - m), d), t)[1], 0)

    def far_contribute(c):
        for d in (0, 1):
            for h in range(heads):
                hs = pl.ds(h * HEAD_DIM, HEAD_DIM)
                o = cbuf[c, d, :, :, hs] + contribution(c, far_at(d), h, d)
                rs[d, c, half - 1, :, :, hs] = o.astype(jnp.bfloat16)

    def start_sums(c, entries):
        for e in entries:
            for d in (0, 1):
                step_on(d, c, half - 1, e).start()

    def add_on(c, d, m, e):
        sum_arrived(d, c, m, e)
        o = cbuf[c, d, e] + rs[d, c, m, e].astype(jnp.float32)
        rs[d, c, m, e] = o.astype(jnp.bfloat16)
        step_on(d, c, m, e).start()

    def last_sum(c, e):
        sum_arrived(0, c, 0, e)
        sum_arrived(1, c, 0, e)
        o = cbuf[c, 0, e] + (rs[0, c, 0, e].astype(jnp.float32) + rs[1, c, 0, e].astype(jnp.float32))
        fin[c, e] = o.astype(jnp.bfloat16)
        give_back(c, e).start()

    def give_back(c, e):
        return remote(fin.at[c, e], sg_out.at[c, e], f_s.at[c, e], f_r.at[c, e], sibling)

    def attended_span(b, sp):
        y_b = y if b == 0 else 1 - y
        outs = []
        for h in range(heads):
            hs = pl.ds(h * HEAD_DIM, HEAD_DIM)
            acc = jnp.zeros((SPAN, HEAD_DIM), jnp.float32)
            for j in range(NEIGH):
                at = sp * NEIGH + j
                idx = tab_u[b * 3, at]
                sl = idx * SLOTS + tab_u[b * 3 + 1, at]
                es = tab_u[b * 3 + 2, at]
                w = column(wts[j], y_b * ch + sp + h * stride)
                p = (pb[sl, :, hs] * w).astype(jnp.bfloat16)
                near = jnp.dot(p, kv[1, idx, es, :, hs], preferred_element_type=jnp.float32)
                away = far_a[1, b, lax.rem(tab_u[b * 3 + 1, at], 2), :, hs].astype(jnp.float32)
                acc += jnp.where(idx == half, away, near)
            outs.append((hs, acc))
        return outs

    def nbr_span(sp, t):
        for hs, acc in attended_span(1, sp):
            asend[sp, :, hs] = acc.astype(jnp.bfloat16)
        return t

    def own_span(sp, t):
        for hs, acc in attended_span(0, sp):
            both = acc + arecv[sp, :, hs].astype(jnp.float32)
            att[sp, :, hs] = both.astype(jnp.bfloat16)
        return t

    give = remote(asend, arecv, a_s.at[0], a_r.at[0], y_nbr)
    out_copy = pltpu.make_async_copy(att, att_out, o_l.at[0])

    contribute_both(1, half - 1)
    if half > 2:
        pass_on(1, half - 2, 2)
    for f in (0, 1):
        far_tile(2, f).wait_recv()
    far_contribute(1)
    for b in (0, 1):
        items(grad_item, nbr_at, upto(half - 2), b)
    start_sums(1, (0,))
    for e in range(3):
        pass_on(1, half - 1, e)
    far_send(1, far_slot(grad_slot, far_g))
    start_sums(1, (1,))
    if half > 2:
        contribute_both(1, half - 2)
        for d in (0, 1):
            add_on(1, d, half - 2, 0)
    for b in (0, 1):
        items(grad_item, upto(half - 2), upto(half - 1), b)
    far_insert(1, gp)
    gc = wts[0] * gp[0] + wts[1] * gp[1]
    stats.append(exchange(1, gc))
    dlt[...] = gc + st_r[1]
    far_send(3, lambda b, r: [
        column(dlt[...], jnp.maximum(*slot_lanes(half, b * 2 + r, h))) for h in range(heads)])
    start_sums(1, (2,))
    contribute_both(0, half - 1)

    for f in (0, 1):
        for r in (0, 1):
            for h in range(heads):
                hs = pl.ds(h * HEAD_DIM, HEAD_DIM)
                p = (pb[half * SLOTS + f * 2 + r, :, hs] * far_get(2, f, r, h)).astype(jnp.bfloat16)
                o = jnp.dot(p, kv[1, far_at(f), far_entry(f, r), :, hs],
                            preferred_element_type=jnp.float32)
                far_a[0, f, r, :, hs] = o.astype(jnp.bfloat16)
    for f in (0, 1):
        far_tile(3, f).wait_recv()
    far_contribute(0)
    start_sums(0, (0, 1, 2))
    for f in (0, 1):
        far_part(f).start()

    def spans(k):
        if half < 8:
            return

        @pl.when(k == 2)
        def _():
            for f in (0, 1):
                far_part(f).wait_recv()

        @pl.when(k <= 3)
        def _():
            lax.fori_loop((k - 2) * (ch // 2), (k - 1) * (ch // 2), nbr_span, 0)

        @pl.when(k == 3)
        def _():
            give.start()

        @pl.when(k == 6)
        def _():
            give.wait_recv()

        @pl.when(jnp.logical_and(k >= 6, k <= 7))
        def _():
            lax.fori_loop((k - 6) * (ch // 2), (k - 5) * (ch // 2), own_span, 0)

        @pl.when(k == 7)
        def _():
            out_copy.start()

    def early_sent(c):
        for d in (0, 1):
            for e in range(3):
                first(d, c, e).wait_send()
                lax.fori_loop(2, half, lambda k, t: (forward(d, c, k, e).wait_send(), t)[1], 0)

    def small_sent():
        for b in (0, 1):
            for copy in ([far_spans(0, b), far_spans(1, b), far_table(b), far_part(b)]
                         + [far_tile(i, b) for i in range(4)]):
                copy.wait_send()
        for copy in locals_ + swap + maps + stats + [give]:
            copy.wait_send()

    def sums_sent(m):
        for c in (0, 1):
            for d in (0, 1):
                for e in range(3):
                    step_on(d, c, m, e).wait_send()

    def sum_step(k, t):
        m = half - k
        pl.when(k > 2)(lambda: contribute_both(1, m))
        contribute_both(0, m)

        @pl.when(k > 2)
        def _():
            for d in (0, 1):
                add_on(1, d, m, 0)

        for e in range(3):
            for c in (1, 0):
                if c == 0 or e > 0:
                    for d in (0, 1):
                        add_on(c, d, m, e)
        spans(k)
        if half >= 8:
            pl.when(k == 4)(lambda: early_sent(0))
            pl.when(k == 5)(lambda: early_sent(1))
            pl.when(k == 7)(small_sent)

        @pl.when(k >= 3)
        def _():
            sums_sent(m + 2)

        return t

    lax.fori_loop(2, half, sum_step, 0)
    if half < 8:
        for f in (0, 1):
            far_part(f).wait_recv()
        lax.fori_loop(0, ch, nbr_span, 0)
        give.start()
        give.wait_recv()
        lax.fori_loop(0, ch, own_span, 0)
        out_copy.start()
    contribute(1, 0, 0)
    contribute(0, 0, 0)
    for e in range(3):
        for c in (1, 0):
            last_sum(c, e)

    if half < 8:
        early_sent(0)
        early_sent(1)
        small_sent()
    for m in sorted({1, min(2, half - 1)}):
        sums_sent(m)
    for c in (0, 1):
        for e in range(3):
            give_back(c, e).wait_send()
            give_back(c, e).wait_recv()
    out_copy.wait()


def place_results(att_in, sums_in, att_out, sums_out, att, sums, in_sem, out_sem):
    size = att_in.shape[0] // PIECES
    parts = [[ref.at[pl.ds(i * size, size)] for ref in (att_in, att, att_out)]
             for i in range(PIECES)]
    parts += [[ref.at[c] for ref in (sums_in, sums, sums_out)] for c in range(2)]
    loads = [pltpu.make_async_copy(a, b, in_sem.at[i]) for i, (a, b, _) in enumerate(parts)]
    stores = [pltpu.make_async_copy(b, c, out_sem.at[i]) for i, (_, b, c) in enumerate(parts)]
    for copy in loads:
        copy.start()
    for load, store in zip(loads, stores):
        load.wait()
        store.start()
    for copy in stores:
        copy.wait()


def per_device(nz, queries, store_kv, out_grad, neighbour_owner, neighbour_slot, neighbour_count):
    rows, width = queries.shape
    heads = width // HEAD_DIM
    ch = rows // SPAN
    half = nz // 2
    entries = store_kv.shape[1] // NLEN
    nt = lax.axis_size("tensor")
    bf, f32 = jnp.bfloat16, jnp.float32
    dma = pltpu.SemaphoreType.DMA
    block = (entries, NLEN, width)
    spans = (ch, SPAN, width)
    any_spec = pl.BlockSpec(memory_space=pl.ANY)
    attended, store_grad = pl.pallas_call(
        functools.partial(kernel, nz, nt, ch, heads),
        out_shape=[jax.ShapeDtypeStruct(spans, bf), jax.ShapeDtypeStruct((2,) + block, bf)],
        in_specs=[pl.BlockSpec(memory_space=pltpu.SMEM)] * 3 + [any_spec, any_spec, any_spec],
        out_specs=[any_spec, any_spec],
        scratch_shapes=[
            pltpu.VMEM((2, nz) + block, bf),
            pltpu.VMEM(spans, bf), pltpu.VMEM(spans, bf),
            pltpu.VMEM(spans, bf), pltpu.VMEM(spans, bf),
            pltpu.VMEM((nz * SLOTS, SPAN, width), f32),
            pltpu.VMEM((nz * SLOTS, SPAN, width), f32),
            pltpu.VMEM((2, 2, half + 1) + block, bf),
            pltpu.VMEM((2, 2) + block, f32),
            pltpu.VMEM((2,) + block, bf),
            pltpu.VMEM(spans, bf), pltpu.VMEM(spans, bf), pltpu.VMEM(spans, bf),
            pltpu.VMEM((2, SPAN, 128), f32), pltpu.VMEM((2, SPAN, 128), f32),
            pltpu.VMEM((2, SPAN, 128), f32), pltpu.VMEM((2, SPAN, 128), f32),
            pltpu.VMEM((2, SPAN, 128), f32), pltpu.VMEM((SPAN, 128), f32),
            dma((2, 2, half + 1, 3)), dma((2, 2, half + 1, 3)), dma((2,)), dma((2,)),
            dma((2,)), dma((2,)), dma((2,)), dma((2,)), dma((2,)),
            dma((2, 2, half + 1, 3)), dma((2, 2, half + 1, 3)), dma((1,)), dma((1,)),
            dma((2, 3)), dma((2, 3)), dma((1,)),
            pltpu.VMEM((2, nt, 8, 128), jnp.int32), pltpu.VMEM((nz, 128), jnp.int32),
            pltpu.VMEM((8, 128), jnp.int32), pltpu.SMEM((nz, 128), jnp.int32),
            pltpu.SMEM((8, 128), jnp.int32), dma((2, nt)), dma((2, nt)), dma((2,)),
            pltpu.VMEM((2, 2, 2, SPAN, width), bf), pltpu.VMEM((2, 2, 2, SPAN, width), bf),
            pltpu.VMEM((2, nz, 128), jnp.int32), pltpu.SMEM((2, nz, 128), jnp.int32),
            pltpu.VMEM((2, 4, 2, SPAN, 128), f32), pltpu.VMEM((2, 2, 2, SPAN, width), bf),
            dma((8, 2)), dma((8, 2)), dma((2,)),
        ],
        compiler_params=pltpu.CompilerParams(
            collective_id=0, has_side_effects=True, vmem_limit_bytes=60 * 1024 * 1024),
        cost_estimate=pl.CostEstimate(flops=4 * 10 ** 9, bytes_accessed=6 * 10 ** 6,
                                      transcendentals=4 * 10 ** 6),
    )(neighbour_owner, neighbour_slot, neighbour_count, queries.reshape(spans), store_kv.reshape((2,) + block), out_grad.reshape(spans))
    attended, store_grad = pl.pallas_call(
        place_results,
        out_shape=[jax.ShapeDtypeStruct(spans, bf), jax.ShapeDtypeStruct((2,) + block, bf)],
        in_specs=[any_spec, any_spec],
        out_specs=[any_spec, any_spec],
        scratch_shapes=[pltpu.VMEM(spans, bf), pltpu.VMEM((2,) + block, bf),
                        dma((PIECES + 2,)), dma((PIECES + 2,))],
        compiler_params=pltpu.CompilerParams(vmem_limit_bytes=60 * 1024 * 1024),
    )(attended, store_grad)
    return attended.reshape(rows, width), store_grad.reshape(store_kv.shape)


def solution(mesh):
    nz = mesh.shape["seq"] // 2
    in_specs = (
        P(("section", "seq"), "tensor"),
        P(None, ("section", "seq"), "tensor"),
        P(("section", "seq"), "tensor"),
        P(("section", "seq", "tensor"), None),
        P(("section", "seq", "tensor"), None),
        P(("section", "seq", "tensor")),
    )
    out_specs = (P(("section", "seq"), "tensor"), P(None, ("section", "seq"), "tensor"))
    return jax.shard_map(
        functools.partial(per_device, nz), mesh=mesh, in_specs=in_specs, out_specs=out_specs,
        check_vma=False)
```

```python
import functools

import jax
import jax.numpy as jnp
from jax import lax
from jax.experimental import pallas as pl
from jax.experimental.pallas import tpu as pltpu
from jax.sharding import PartitionSpec as P

HEAD_DIM = 128
SPAN = 64
NLEN = 128
NEIGH = 2
SLOTS = 4
MESH = pl.DeviceIdType.MESH
DEAD = -1e30
NONE = -100000
PIECES = 4


def kernel(nz, nt, ch, heads, owner_in, entry_in, count_in, q_in, kv_in, g_in, att_out, sg_out,
           kv, q_own, q_nbr, g_own, g_nbr, pb, dpb, rs, cbuf, fin, asend, arecv, att,
           lse, gp, st_s, st_r, wts, dlt,
           ag_s, ag_r, loc_s, loc_r, qg_s, qg_r, own_l, stx_s, stx_r,
           rs_s, rs_r, a_s, a_r, f_s, f_r, o_l,
           meta, made, made_u, tab, tab_u, me_s, me_r, t_l,
           far_q, far_g, far_made, far_tab, far_st, far_a, fx_s, fx_r, ft_l):
    half = nz // 2
    stride = 2 * ch
    per_t = ch // nt
    scaling = HEAD_DIM ** (-0.5)
    q_blk, g_blk = (q_own, q_nbr), (g_own, g_nbr)
    sec = lax.axis_index("section")
    seq = lax.axis_index("seq")
    ten = lax.axis_index("tensor")
    y, z = lax.div(seq, nz), lax.rem(seq, nz)
    up, down = lax.rem(z + 1, nz), lax.rem(z + nz - 1, nz)
    z_to = (up, down)

    def dev(s, yy, zz):
        return {"section": s, "seq": yy * nz + zz}

    sibling = dev(1 - sec, y, z)
    y_nbr = dev(sec, 1 - y, z)

    def peer(b, dt):
        return {"seq": (y if b == 0 else 1 - y) * nz + z, "tensor": lax.rem(ten + dt, nt)}

    def remote(src, dst, ssem, rsem, device):
        return pltpu.make_async_remote_copy(
            src_ref=src, dst_ref=dst, send_sem=ssem, recv_sem=rsem,
            device_id=device, device_id_type=MESH)

    barrier = pltpu.get_barrier_semaphore()
    for device in (sibling, y_nbr, dev(sec, y, up), dev(sec, y, down),
                   dev(1 - sec, y, up), dev(1 - sec, y, down)) + tuple(
                       peer(b, dt) for b in (0, 1) for dt in range(1, nt)):
        pl.semaphore_signal(barrier, inc=1, device_id=device, device_id_type=MESH)
    own_q = pltpu.make_async_copy(q_in, q_own, own_l.at[0])
    own_g = pltpu.make_async_copy(g_in, g_own, own_l.at[1])
    own_q.start()
    own_g.start()
    lanes8 = lax.broadcasted_iota(jnp.int32, (8, 128), 1)
    rows8 = lax.broadcasted_iota(jnp.int32, (8, 128), 0)
    mine = jnp.zeros((8, 128), jnp.int32)
    for s in range(per_t):
        for j in range(NEIGH):
            at = lanes8 == (ten * per_t + s) * NEIGH + j
            for row, value in enumerate((owner_in[s, j], entry_in[s, j], count_in[s])):
                mine = jnp.where(jnp.logical_and(at, rows8 == row), value, mine)
    meta[0, ten] = mine
    pl.semaphore_wait(barrier, 6 + 2 * (nt - 1))

    def place(d, k):
        return nz - k if d == 0 else k

    def first(d, c, e):
        return remote(kv_in.at[c, e], kv.at[c, place(d, 1), e], ag_s.at[d, c, 1, e],
                      ag_r.at[d, c, 1, e], dev(1 - sec, y, z_to[d]))

    def forward(d, c, k, e):
        return remote(kv.at[c, place(d, k - 1), e], kv.at[c, place(d, k), e], ag_s.at[d, c, k, e],
                      ag_r.at[d, c, k, e], dev(sec, y, z_to[d]))

    def arrived(d, c, k, e):
        here = kv.at[c, place(d, k), e]
        remote(here, here, ag_s.at[d, c, k, e], ag_r.at[d, c, k, e],
               dev(sec, y, z_to[d])).wait_recv()

    def pass_on(c, k, e):
        for d in (0, 1):
            arrived(d, c, k, e)
            if not isinstance(k, int) or k < half - 1:
                forward(d, c, k + 1, e).start()

    def start_gather():
        for e in range(3):
            for c in (0, 1):
                for d in (0, 1):
                    first(d, c, e).start()

    start_gather()
    locals_ = [remote(kv_in.at[c], kv.at[c, 0], loc_s.at[c], loc_r.at[c], sibling) for c in (0, 1)]
    for copy in locals_:
        copy.start()
    maps = [remote(meta.at[0, ten], meta.at[b, ten], me_s.at[b, dt], me_r.at[b, dt],
                   peer(b, dt)) for dt in range(nt) for b in (0, 1) if b + dt > 0]
    for copy in maps:
        copy.start()
    swap = [remote(q_in, q_nbr, qg_s.at[0], qg_r.at[0], y_nbr),
            remote(g_in, g_nbr, qg_s.at[1], qg_r.at[1], y_nbr)]
    for copy in swap:
        copy.start()

    lse[...] = jnp.full_like(lse, DEAD)
    gp[...] = jnp.zeros_like(gp)
    lanes = lax.broadcasted_iota(jnp.int32, (SPAN, 128), 1)

    def build_tables():
        for dt in range(nt):
            for b in (0, 1):
                if b + dt > 0:
                    here = meta.at[b, lax.rem(ten + nt - dt, nt)]
                    remote(here, here, me_s.at[b, dt], me_r.at[b, dt], peer(b, dt)).wait_recv()
        unit = lax.broadcasted_iota(jnp.int32, (nz, 128), 1)
        row = lax.broadcasted_iota(jnp.int32, (nz, 128), 0)
        made_all = jnp.zeros((nz, 128), jnp.int32)
        unit_all = jnp.zeros((8, 128), jnp.int32)
        for b in (0, 1):
            whole = meta[b, 0]
            for t in range(1, nt):
                whole = whole + meta[b, t]
            spread = lambda i: jnp.broadcast_to(whole[i:i + 1], (nz, 128))
            owner, entry, count = spread(0), spread(1), spread(2)
            j_of = lax.bitwise_and(unit, 1)
            span = lax.shift_right_logical(unit, 1)
            col = owner - y * nz
            used = ((unit < ch * NEIGH) & (j_of < count)) & ((col >= 0) & (col < nz))
            rel = jnp.where(col < z, col - z + nz, col - z)
            mine = jnp.logical_and(used, rel == row)
            u0 = jnp.min(jnp.where(mine, unit, 1000), axis=1, keepdims=True)
            u1 = jnp.max(jnp.where(mine, unit, -1), axis=1, keepdims=True)
            u1 = jnp.where(u1 == u0, -1, u1)
            lane = (y if b == 0 else 1 - y) * ch + span
            for r, u in ((0, u0), (1, u1)):
                at = unit == u
                get = lambda v: jnp.sum(jnp.where(at, v, 0), axis=1, keepdims=True)
                values = (get(span), get(entry)) + tuple(
                    get(jnp.where(j_of == j, lane - NONE, 0)) + NONE for j in range(NEIGH))
                for i, value in enumerate(values):
                    made_all = jnp.where(unit == i * SLOTS + b * 2 + r, value, made_all)
            rank = jnp.sum(jnp.where(jnp.logical_and(mine, unit != u0), 1, 0), axis=0, keepdims=True)
            use1, rel1, entry1 = used[0:1], rel[0:1], entry[0:1]
            for i, value in enumerate((rel1, b * 2 + rank, entry1)):
                value = jnp.broadcast_to(jnp.where(use1, value, 0), (8, 128))
                unit_all = jnp.where(rows8 == b * 3 + i, value, unit_all)
        made[...] = made_all
        made_u[...] = unit_all
        copies = [pltpu.make_async_copy(made, tab, t_l.at[0]),
                  pltpu.make_async_copy(made_u, tab_u, t_l.at[1])]
        for copy in copies:
            copy.start()
        for copy in copies:
            copy.wait()

    def pick(three, es):
        return jnp.where(es == 0, three[0], jnp.where(es == 1, three[1], three[2]))

    def far_at(f):
        return half - 1 + 2 * f

    def far_copy(i, b, src, dst, back):
        return remote(src, dst, fx_s.at[i, b], fx_r.at[i, b],
                      dev(sec, y, z_to[1 - b] if back else z_to[b]))

    def far_spans(i, b):
        ref = (far_q, far_g)[i]
        return far_copy(i, b, ref.at[0, b], ref.at[1, b], False)

    def far_table(b):
        return far_copy(2, b, made, far_made.at[b], False)

    def far_tile(i, b):
        return far_copy(3 + i, b, far_st.at[0, i, b], far_st.at[1, i, b], i < 2)

    def far_part(b):
        return far_copy(7, b, far_a.at[0, b], far_a.at[1, b], True)

    def send_far():
        for b in (0, 1):
            for r in (0, 1):
                sp = tab[half, b * 2 + r]
                far_q[0, b, r] = q_blk[b][sp]
                far_g[0, b, r] = g_blk[b][sp]
        for b in (0, 1):
            far_table(b).start()
            far_spans(0, b).start()
            far_spans(1, b).start()

    def take_far():
        for b in (0, 1):
            far_table(b).wait_recv()
            pltpu.make_async_copy(far_made.at[b], far_tab.at[b], ft_l.at[b]).start()
        for b in (0, 1):
            pltpu.make_async_copy(far_made.at[b], far_tab.at[b], ft_l.at[b]).wait()
            far_spans(0, b).wait_recv()
            far_spans(1, b).wait_recv()

    def far_send(i, work):
        for f in (0, 1):
            tile = jnp.zeros((SPAN, 128), jnp.float32)
            for r in (0, 1):
                for h, value in enumerate(work(f, r)):
                    tile = jnp.where(lanes == r * heads + h, value, tile)
            far_st[0, i, f] = tile
            far_tile(i, f).start()

    def column(values, lane):
        return jnp.sum(jnp.where(lanes == lane, values, 0.0), axis=1, keepdims=True)

    def far_get(i, f, r, h):
        return column(far_st[1, i, f], r * heads + h)

    def far_insert(i, ref):
        for b in (0, 1):
            far_tile(i, b).wait_recv()
            for r in (0, 1):
                insert(ref, half, b * 2 + r, [far_get(i, b, r, h) for h in range(heads)])

    def place_of(n):
        return jnp.where(lax.rem(n, 2) == 1, nz - lax.div(n + 1, 2), lax.div(n, 2))

    def insert(ref, idx, slot, columns):
        for j in range(NEIGH):
            lane = tab[idx, (2 + j) * SLOTS + slot]
            a = ref[j]
            for h in range(heads):
                a = jnp.where(lanes == lane + h * stride, columns[h], a)
            ref[j] = a

    def score_slot(idx, sl, es, q_of):
        columns = []
        for h in range(heads):
            hs = pl.ds(h * HEAD_DIM, HEAD_DIM)
            ks = pick([kv[0, idx, e, :, hs] for e in range(3)], es)
            s = lax.dot_general(q_of(hs), ks, (((1,), (1,)), ((), ())),
                                preferred_element_type=jnp.float32) * scaling
            top = jnp.max(s, axis=1, keepdims=True)
            p = jnp.exp(s - top)
            tot = jnp.sum(p, axis=1, keepdims=True)
            pb[sl, :, hs] = p * (1.0 / tot)
            columns.append(top + jnp.log(tot))
        return columns

    def grad_slot(idx, sl, es, g_of):
        columns = []
        for h in range(heads):
            hs = pl.ds(h * HEAD_DIM, HEAD_DIM)
            vs = pick([kv[1, idx, e, :, hs] for e in range(3)], es)
            dp = lax.dot_general(g_of(hs), vs, (((1,), (1,)), ((), ())),
                                 preferred_element_type=jnp.float32)
            dpb[sl, :, hs] = dp
            columns.append(jnp.sum(pb[sl, :, hs] * dp, axis=1, keepdims=True))
        return columns

    def item(n, b, slot_work, rows, ref):
        idx = place_of(n)
        for r in (0, 1):
            slot = b * 2 + r
            sp = tab[idx, slot]
            insert(ref, idx, slot, slot_work(idx, idx * SLOTS + slot, tab[idx, SLOTS + slot],
                                             lambda hs: rows[b][sp, :, hs]))

    def far_entry(f, r):
        return far_tab[f, half, SLOTS + f * 2 + r]

    def far_slot(slot_work, rows):
        return lambda f, r: slot_work(far_at(f), half * SLOTS + f * 2 + r, far_entry(f, r),
                                      lambda hs: rows[1, f, r, :, hs])

    def score_item(n, b):
        item(n, b, score_slot, q_blk, lse)

    def grad_item(n, b):
        item(n, b, grad_slot, g_blk, gp)

    def items(work, lo, hi, b):
        lax.fori_loop(lo, hi, lambda n, t: (work(n, b), t)[1], 0)

    own_q.wait()
    own_g.wait()
    for copy in locals_:
        copy.wait_recv()
    build_tables()
    lag = 4

    def done(k):
        return jnp.maximum((k + 1 - lag) * 4, 0)

    def upto(step):
        return max(2 * step + 1, 0)

    def gather_step(k, t):
        pass_on(0, k, 0)
        items(score_item, jnp.maximum(2 * k - 3, 0), 2 * k - 1, 0)
        pass_on(1, k, 0)

        @pl.when(k == lag)
        def _():
            for copy in swap:
                copy.wait_recv()
            send_far()

        lo, hi = done(k - 1), done(k)
        mid = jnp.minimum(lo + 2, hi)
        items(score_item, lo, mid, 1)
        pass_on(0, k, 1)
        items(score_item, mid, hi, 1)
        pass_on(1, k, 1)
        items(grad_item, lo, hi, 0)
        pass_on(0, k, 2)
        items(grad_item, lo, hi, 1)
        pass_on(1, k, 2)
        return t

    both = half - 4
    lax.fori_loop(1, both + 1, gather_step, 0)
    if both < lag:
        for copy in swap:
            copy.wait_recv()
        send_far()
    own_at = upto(both - 1)
    nbr_at = max((both + 1 - lag) * 4, 0)
    for k in range(max(half - 3, 1), half - 1):
        for e in range(3):
            pass_on(0, k, e)
    if half > 3:
        pass_on(1, half - 3, 0)
    for b in (0, 1):
        items(score_item, own_at if b == 0 else nbr_at, upto(half - 2), b)
    take_far()
    for e in range(3):
        pass_on(0, half - 1, e)
    far_send(0, far_slot(score_slot, far_q))
    if half > 3:
        pass_on(1, half - 3, 1)
        pass_on(1, half - 3, 2)
    for b in (0, 1):
        items(score_item, upto(half - 2), upto(half - 1), b)
    far_insert(0, lse)

    def exchange(i, value):
        st_s[i] = value
        copy = remote(st_s.at[i], st_r.at[i], stx_s.at[i], stx_r.at[i], y_nbr)
        copy.start()
        copy.wait_recv()
        return copy

    a0, a1 = lse[0], lse[1]
    top = jnp.maximum(a0, a1)
    lc = top + jnp.log(jnp.exp(a0 - top) + jnp.exp(a1 - top))
    stats = [exchange(0, lc)]
    lo_ = st_r[0]
    top = jnp.maximum(lc, lo_)
    total = top + jnp.log(jnp.exp(lc - top) + jnp.exp(lo_ - top))
    wts[0] = jnp.exp(a0 - total)
    wts[1] = jnp.exp(a1 - total)

    def slot_lanes(idx, slot, h):
        return (tab[idx, 2 * SLOTS + slot] + h * stride, tab[idx, 3 * SLOTS + slot] + h * stride)

    def weight(lane0, lane1):
        w = jnp.where(lanes == lane0, wts[0], 0.0) + jnp.where(lanes == lane1, wts[1], 0.0)
        return jnp.sum(w, axis=1, keepdims=True)

    far_send(2, lambda b, r: [weight(*slot_lanes(half, b * 2 + r, h)) for h in range(heads)])
    if half > 2:
        pass_on(1, half - 2, 0)
        pass_on(1, half - 2, 1)

    def contribution(c, idx, h, f=None):
        hs = pl.ds(h * HEAD_DIM, HEAD_DIM)
        left, right = [], []
        for slot in range(SLOTS) if f is None else range(SLOTS, SLOTS + 2):
            if slot < SLOTS:
                sl = idx * SLOTS + slot
                sp, es = tab[idx, slot], tab[idx, SLOTS + slot]
                l0, l1 = slot_lanes(idx, slot, h)
                w = weight(l0, l1)
                rows = (q_blk, g_blk)[c][slot // 2][sp, :, hs]
            else:
                r = slot - SLOTS
                sl = half * SLOTS + f * 2 + r
                es = far_entry(f, r)
                w = far_get(2, f, r, h)
                rows = (far_q, far_g)[c][1, f, r, :, hs]
            p = pb[sl, :, hs] * w
            if c == 0:
                delta = (column(dlt[...], jnp.maximum(l0, l1)) if slot < SLOTS
                         else far_get(3, f, r, h))
                p = p * (dpb[sl, :, hs] - delta)
            right.append(rows)
            x = p.astype(jnp.bfloat16)
            zero = jnp.zeros_like(x)
            left.append(jnp.concatenate([jnp.where(es == e, x, zero) for e in range(3)], axis=1))
        out = lax.dot_general(jnp.concatenate(left, axis=0), jnp.concatenate(right, axis=0),
                              (((0,), (0,)), ((), ())), preferred_element_type=jnp.float32)
        if c == 0:
            out = out * scaling
        return out.reshape(3, NLEN, HEAD_DIM)

    def contribute(c, idx, into):
        for h in range(heads):
            cbuf[c, into, :, :, pl.ds(h * HEAD_DIM, HEAD_DIM)] = contribution(c, idx, h)

    def step_on(d, c, m, e):
        return remote(rs.at[d, c, m, e], rs.at[d, c, m - 1, e], rs_s.at[d, c, m - 1, e],
                      rs_r.at[d, c, m - 1, e], dev(sec, y, z_to[d]))

    def sum_arrived(d, c, m, e):
        here = rs.at[d, c, m, e]
        remote(here, here, rs_s.at[d, c, m, e], rs_r.at[d, c, m, e], y_nbr).wait_recv()

    def contribute_both(c, m):
        lax.fori_loop(0, 2, lambda d, t: (contribute(c, jnp.where(d == 0, m, nz - m), d), t)[1], 0)

    def far_contribute(c):
        for d in (0, 1):
            for h in range(heads):
                hs = pl.ds(h * HEAD_DIM, HEAD_DIM)
                o = cbuf[c, d, :, :, hs] + contribution(c, far_at(d), h, d)
                rs[d, c, half - 1, :, :, hs] = o.astype(jnp.bfloat16)

    def start_sums(c, entries):
        for e in entries:
            for d in (0, 1):
                step_on(d, c, half - 1, e).start()

    def add_on(c, d, m, e):
        sum_arrived(d, c, m, e)
        o = cbuf[c, d, e] + rs[d, c, m, e].astype(jnp.float32)
        rs[d, c, m, e] = o.astype(jnp.bfloat16)
        step_on(d, c, m, e).start()

    def last_sum(c, e):
        sum_arrived(0, c, 0, e)
        sum_arrived(1, c, 0, e)
        o = cbuf[c, 0, e] + (rs[0, c, 0, e].astype(jnp.float32) + rs[1, c, 0, e].astype(jnp.float32))
        fin[c, e] = o.astype(jnp.bfloat16)
        give_back(c, e).start()

    def give_back(c, e):
        return remote(fin.at[c, e], sg_out.at[c, e], f_s.at[c, e], f_r.at[c, e], sibling)

    def attended_span(b, sp):
        y_b = y if b == 0 else 1 - y
        outs = []
        for h in range(heads):
            hs = pl.ds(h * HEAD_DIM, HEAD_DIM)
            acc = jnp.zeros((SPAN, HEAD_DIM), jnp.float32)
            for j in range(NEIGH):
                at = sp * NEIGH + j
                idx = tab_u[b * 3, at]
                sl = idx * SLOTS + tab_u[b * 3 + 1, at]
                es = tab_u[b * 3 + 2, at]
                w = column(wts[j], y_b * ch + sp + h * stride)
                p = (pb[sl, :, hs] * w).astype(jnp.bfloat16)
                near = jnp.dot(p, kv[1, idx, es, :, hs], preferred_element_type=jnp.float32)
                away = far_a[1, b, lax.rem(tab_u[b * 3 + 1, at], 2), :, hs].astype(jnp.float32)
                acc += jnp.where(idx == half, away, near)
            outs.append((hs, acc))
        return outs

    def nbr_span(sp, t):
        for hs, acc in attended_span(1, sp):
            asend[sp, :, hs] = acc.astype(jnp.bfloat16)
        return t

    def own_span(sp, t):
        for hs, acc in attended_span(0, sp):
            both = acc + arecv[sp, :, hs].astype(jnp.float32)
            att[sp, :, hs] = both.astype(jnp.bfloat16)
        return t

    give = remote(asend, arecv, a_s.at[0], a_r.at[0], y_nbr)
    out_copy = pltpu.make_async_copy(att, att_out, o_l.at[0])

    contribute_both(1, half - 1)
    if half > 2:
        pass_on(1, half - 2, 2)
    for f in (0, 1):
        far_tile(2, f).wait_recv()
    far_contribute(1)
    start_sums(1, (0,))
    for b in (0, 1):
        items(grad_item, nbr_at, upto(half - 2), b)
    for e in range(3):
        pass_on(1, half - 1, e)
    far_send(1, far_slot(grad_slot, far_g))
    start_sums(1, (1,))
    if half > 2:
        contribute_both(1, half - 2)
        for d in (0, 1):
            add_on(1, d, half - 2, 0)
    for b in (0, 1):
        items(grad_item, upto(half - 2), upto(half - 1), b)
    far_insert(1, gp)
    gc = wts[0] * gp[0] + wts[1] * gp[1]
    stats.append(exchange(1, gc))
    dlt[...] = gc + st_r[1]
    far_send(3, lambda b, r: [
        column(dlt[...], jnp.maximum(*slot_lanes(half, b * 2 + r, h))) for h in range(heads)])
    start_sums(1, (2,))
    contribute_both(0, half - 1)

    for f in (0, 1):
        for r in (0, 1):
            for h in range(heads):
                hs = pl.ds(h * HEAD_DIM, HEAD_DIM)
                p = (pb[half * SLOTS + f * 2 + r, :, hs] * far_get(2, f, r, h)).astype(jnp.bfloat16)
                o = jnp.dot(p, kv[1, far_at(f), far_entry(f, r), :, hs],
                            preferred_element_type=jnp.float32)
                far_a[0, f, r, :, hs] = o.astype(jnp.bfloat16)
    for f in (0, 1):
        far_tile(3, f).wait_recv()
    far_contribute(0)
    start_sums(0, (0, 1, 2))
    for f in (0, 1):
        far_part(f).start()

    def spans(k):
        if half < 8:
            return

        @pl.when(k == 2)
        def _():
            for f in (0, 1):
                far_part(f).wait_recv()

        @pl.when(k <= 3)
        def _():
            lax.fori_loop((k - 2) * (ch // 2), (k - 1) * (ch // 2), nbr_span, 0)

        @pl.when(k == 3)
        def _():
            give.start()

        @pl.when(k == 6)
        def _():
            give.wait_recv()

        @pl.when(jnp.logical_and(k >= 6, k <= 7))
        def _():
            lax.fori_loop((k - 6) * (ch // 2), (k - 5) * (ch // 2), own_span, 0)

        @pl.when(k == 7)
        def _():
            out_copy.start()

    def early_sent(c):
        for d in (0, 1):
            for e in range(3):
                first(d, c, e).wait_send()
                lax.fori_loop(2, half, lambda k, t: (forward(d, c, k, e).wait_send(), t)[1], 0)

    def small_sent():
        for b in (0, 1):
            for copy in ([far_spans(0, b), far_spans(1, b), far_table(b), far_part(b)]
                         + [far_tile(i, b) for i in range(4)]):
                copy.wait_send()
        for copy in locals_ + swap + maps + stats + [give]:
            copy.wait_send()

    def sums_sent(m):
        for c in (0, 1):
            for d in (0, 1):
                for e in range(3):
                    step_on(d, c, m, e).wait_send()

    def sum_step(k, t):
        m = half - k
        pl.when(k > 2)(lambda: contribute_both(1, m))
        contribute_both(0, m)

        @pl.when(k > 2)
        def _():
            for d in (0, 1):
                add_on(1, d, m, 0)

        for e in range(3):
            for c in (1, 0):
                if c == 0 or e > 0:
                    for d in (0, 1):
                        add_on(c, d, m, e)
        spans(k)
        if half >= 8:
            pl.when(k == 4)(lambda: early_sent(0))
            pl.when(k == 5)(lambda: early_sent(1))
            pl.when(k == 7)(small_sent)

        @pl.when(k >= 3)
        def _():
            sums_sent(m + 2)

        return t

    lax.fori_loop(2, half, sum_step, 0)
    if half < 8:
        for f in (0, 1):
            far_part(f).wait_recv()
        lax.fori_loop(0, ch, nbr_span, 0)
        give.start()
        give.wait_recv()
        lax.fori_loop(0, ch, own_span, 0)
        out_copy.start()
    contribute(1, 0, 0)
    contribute(0, 0, 0)
    for e in range(3):
        for c in (1, 0):
            last_sum(c, e)

    if half < 8:
        early_sent(0)
        early_sent(1)
        small_sent()
    for m in sorted({1, min(2, half - 1)}):
        sums_sent(m)
    for c in (0, 1):
        for e in range(3):
            give_back(c, e).wait_send()
            give_back(c, e).wait_recv()
    out_copy.wait()


def place_results(att_in, sums_in, att_out, sums_out, att, sums, in_sem, out_sem):
    size = att_in.shape[0] // PIECES
    parts = [[ref.at[pl.ds(i * size, size)] for ref in (att_in, att, att_out)]
             for i in range(PIECES)]
    parts += [[ref.at[c] for ref in (sums_in, sums, sums_out)] for c in range(2)]
    loads = [pltpu.make_async_copy(a, b, in_sem.at[i]) for i, (a, b, _) in enumerate(parts)]
    stores = [pltpu.make_async_copy(b, c, out_sem.at[i]) for i, (_, b, c) in enumerate(parts)]
    for copy in loads:
        copy.start()
    for load, store in zip(loads, stores):
        load.wait()
        store.start()
    for copy in stores:
        copy.wait()


def per_device(nz, queries, store_kv, out_grad, neighbour_owner, neighbour_slot, neighbour_count):
    rows, width = queries.shape
    heads = width // HEAD_DIM
    ch = rows // SPAN
    half = nz // 2
    entries = store_kv.shape[1] // NLEN
    nt = lax.axis_size("tensor")
    bf, f32 = jnp.bfloat16, jnp.float32
    dma = pltpu.SemaphoreType.DMA
    block = (entries, NLEN, width)
    spans = (ch, SPAN, width)
    any_spec = pl.BlockSpec(memory_space=pl.ANY)
    attended, store_grad = pl.pallas_call(
        functools.partial(kernel, nz, nt, ch, heads),
        out_shape=[jax.ShapeDtypeStruct(spans, bf), jax.ShapeDtypeStruct((2,) + block, bf)],
        in_specs=[pl.BlockSpec(memory_space=pltpu.SMEM)] * 3 + [any_spec, any_spec, any_spec],
        out_specs=[any_spec, any_spec],
        scratch_shapes=[
            pltpu.VMEM((2, nz) + block, bf),
            pltpu.VMEM(spans, bf), pltpu.VMEM(spans, bf),
            pltpu.VMEM(spans, bf), pltpu.VMEM(spans, bf),
            pltpu.VMEM((nz * SLOTS, SPAN, width), f32),
            pltpu.VMEM((nz * SLOTS, SPAN, width), f32),
            pltpu.VMEM((2, 2, half + 1) + block, bf),
            pltpu.VMEM((2, 2) + block, f32),
            pltpu.VMEM((2,) + block, bf),
            pltpu.VMEM(spans, bf), pltpu.VMEM(spans, bf), pltpu.VMEM(spans, bf),
            pltpu.VMEM((2, SPAN, 128), f32), pltpu.VMEM((2, SPAN, 128), f32),
            pltpu.VMEM((2, SPAN, 128), f32), pltpu.VMEM((2, SPAN, 128), f32),
            pltpu.VMEM((2, SPAN, 128), f32), pltpu.VMEM((SPAN, 128), f32),
            dma((2, 2, half + 1, 3)), dma((2, 2, half + 1, 3)), dma((2,)), dma((2,)),
            dma((2,)), dma((2,)), dma((2,)), dma((2,)), dma((2,)),
            dma((2, 2, half + 1, 3)), dma((2, 2, half + 1, 3)), dma((1,)), dma((1,)),
            dma((2, 3)), dma((2, 3)), dma((1,)),
            pltpu.VMEM((2, nt, 8, 128), jnp.int32), pltpu.VMEM((nz, 128), jnp.int32),
            pltpu.VMEM((8, 128), jnp.int32), pltpu.SMEM((nz, 128), jnp.int32),
            pltpu.SMEM((8, 128), jnp.int32), dma((2, nt)), dma((2, nt)), dma((2,)),
            pltpu.VMEM((2, 2, 2, SPAN, width), bf), pltpu.VMEM((2, 2, 2, SPAN, width), bf),
            pltpu.VMEM((2, nz, 128), jnp.int32), pltpu.SMEM((2, nz, 128), jnp.int32),
            pltpu.VMEM((2, 4, 2, SPAN, 128), f32), pltpu.VMEM((2, 2, 2, SPAN, width), bf),
            dma((8, 2)), dma((8, 2)), dma((2,)),
        ],
        compiler_params=pltpu.CompilerParams(
            collective_id=0, has_side_effects=True, vmem_limit_bytes=60 * 1024 * 1024),
        cost_estimate=pl.CostEstimate(flops=4 * 10 ** 9, bytes_accessed=6 * 10 ** 6,
                                      transcendentals=4 * 10 ** 6),
    )(neighbour_owner, neighbour_slot, neighbour_count, queries.reshape(spans), store_kv.reshape((2,) + block), out_grad.reshape(spans))
    attended, store_grad = pl.pallas_call(
        place_results,
        out_shape=[jax.ShapeDtypeStruct(spans, bf), jax.ShapeDtypeStruct((2,) + block, bf)],
        in_specs=[any_spec, any_spec],
        out_specs=[any_spec, any_spec],
        scratch_shapes=[pltpu.VMEM(spans, bf), pltpu.VMEM((2,) + block, bf),
                        dma((PIECES + 2,)), dma((PIECES + 2,))],
        compiler_params=pltpu.CompilerParams(vmem_limit_bytes=60 * 1024 * 1024),
    )(attended, store_grad)
    return attended.reshape(rows, width), store_grad.reshape(store_kv.shape)


def solution(mesh):
    nz = mesh.shape["seq"] // 2
    in_specs = (
        P(("section", "seq"), "tensor"),
        P(None, ("section", "seq"), "tensor"),
        P(("section", "seq"), "tensor"),
        P(("section", "seq", "tensor"), None),
        P(("section", "seq", "tensor"), None),
        P(("section", "seq", "tensor")),
    )
    out_specs = (P(("section", "seq"), "tensor"), P(None, ("section", "seq"), "tensor"))
    return jax.shard_map(
        functools.partial(per_device, nz), mesh=mesh, in_specs=in_specs, out_specs=out_specs,
        check_vma=False)
```
